128 devices in a mesh: dp: 32 (over z, y, core), tensor: 4 (over x).
Axes of the slice: x: 4, y: 4, z: 4, core: 2. Of those that a mesh axis runs over, the one named last changes fastest.
Arguments:
- tokens: float32 [16384, 1024], P(('dp', 'tensor')), may hold values from -6 to 6
- cotangent: float32 [16384, 1024], P(('dp', 'tensor')), may hold values from -6 to 6
- matrices: float32 [2, 12, 1024, 1024], P(None, None, 'dp', 'tensor')
- vectors: float32 [2, 12, 1024], replicated
- first_moment: float32 [2, 12, 1024], replicated, may hold values from -80 to 80
- second_moment: float32 [2, 12, 1024], replicated, may hold values from 862 to 3276
- momenta: float32 [32, 1024, 1024], P('dp', None, 'tensor')
- lengths: int32 [64], replicated, may hold values from 1 to 512, as said below
- assign: int32 [64], replicated, may hold values from 0 to 31, as said below
- owner_slots: int32 [24], replicated, may hold values from 0 to 31, as said below
Outputs:
- out_tokens: float32 [16384, 1024], P(('dp', 'tensor'))
- grad_tokens: float32 [16384, 1024], P(('dp', 'tensor'))
- grad_matrices: float32 [2, 12, 1024, 1024], P(None, None, 'dp', 'tensor')
- new_matrices: float32 [2, 12, 1024, 1024], P(None, None, 'dp', 'tensor')
- new_momenta: float32 [32, 1024, 1024], P('dp', None, 'tensor')
- grad_vectors: float32 [2, 12, 1024], replicated
- new_first: float32 [2, 12, 1024], replicated
- new_second: float32 [2, 12, 1024], replicated
- new_vectors: float32 [2, 12, 1024], replicated
- momentum_scales: float32 [32], P('dp')
The draws below stay inside these ranges and needn't reach their ends.
Inputs may be any that keep to these rules, and one draw needn't show every extreme that they name: `assign`: each dp index holds 1 to 4 sequences, every index at least one. `lengths`: the sequences of one dp index fill at most 512 rows together; some dp index holds a single sequence of exactly 512 rows. All values differ; block n is owned by dp index owner_slots[n].
All inputs are finite; a program needn't handle non-finite values.
Results may differ from the reference program's by a relative error of at most 0.028.
Values may be sent and summed in bfloat16 or wider, within the bound.
A program may use at most 128 MiB of HBM per device.

```python
import math
from functools import partial
import jax
import jax.numpy as jnp
from jax import lax

D = 1024
HEADS = 16
FF = 4096
HEAD_DIM = 64
LAYERS = 2
GROUP = 512
TOKENS = 16384
SEQS = 64
SHORT_MOST = 16
VEC = 12
UNITS = 24
SLOTS = 32
NS_STEPS = 5
STEP = 10
N_DP = 32


def deal_sequences(key):
    groups = SEQS // 2
    key_extra, key_order, key_short, key_long, key_pad, key_full = jax.random.split(key, 6)
    full_group = jax.random.randint(key_full, (), 0, groups)
    extra = jax.random.permutation(key_extra, 3 * (groups - 1))[:groups] // 3
    extra = extra + (extra >= full_group).astype(extra.dtype)
    owners = jnp.concatenate([jnp.arange(groups, dtype=jnp.int32), extra.astype(jnp.int32)])
    owners = owners[jax.random.permutation(key_order, SEQS)]
    shorts = jax.random.randint(key_short, (SEQS,), 1, SHORT_MOST + 1)
    ranking = jax.random.permutation(key_long, SEQS)
    member = owners[:, None] == jnp.arange(groups, dtype=jnp.int32)[None, :]
    best = jnp.max(jnp.where(member, ranking[:, None], -1), axis=0)
    is_long = ranking == best[owners]
    padding = jax.random.randint(key_pad, (groups,), 0, GROUP // 8 + 1)
    padding = jnp.where(jnp.arange(groups) == full_group, 0, padding)
    short_sum = jnp.sum(jnp.where(member & (~is_long)[:, None], shorts[:, None], 0), axis=0)
    long_length = GROUP - padding - short_sum
    seq_lengths = jnp.where(is_long, long_length[owners], shorts).astype(jnp.int32)
    return (seq_lengths, owners.astype(jnp.int32))


def draw_lengths(key, part):
    return deal_sequences(key)[0]


def draw_assign(key, part):
    return deal_sequences(key)[1]


def draw_owner_slots(key, part):
    key = jax.random.fold_in(key, 7)
    key_rest, key_place = jax.random.split(key)
    middle = jax.random.permutation(key_rest, SLOTS - 2)[:UNITS - 2] + 1
    chosen = jnp.concatenate([jnp.array([0, SLOTS - 1], jnp.int32), middle.astype(jnp.int32)])
    return chosen[jax.random.permutation(key_place, UNITS)]


def draw_matrices(key, part):
    key = jax.random.fold_in(key, 3)
    noise = jax.random.normal(key, (LAYERS, VEC, D, D), jnp.float32)
    kinds = jnp.arange(VEC)
    blocks = (VEC - 4) // 2
    scale = jnp.where(kinds == 3, 2.5 * D ** (-0.5), jnp.where(kinds >= 4 + blocks, 1.5 * FF ** (-0.5), D ** (-0.5)))
    return noise * scale[None, :, None, None].astype(jnp.float32)


def draw_vectors(key, part):
    key = jax.random.fold_in(key, 5)
    noise = jnp.clip(jax.random.normal(key, (LAYERS, VEC, D), jnp.float32), -3.0, 3.0)
    kinds = jnp.arange(VEC)
    gains = (kinds == 0) | (kinds == 5)
    return jnp.where(gains[None, :, None], 1.0 + 0.2 * noise, 0.3 * noise)


def draw_momenta(key, part):
    key = jax.random.fold_in(key, 11)
    columns = jnp.arange(D, dtype=jnp.float32) / (D - 1)
    noise = jnp.clip(jax.random.normal(key, (SLOTS, D, D), jnp.float32), -6.0, 6.0)
    top = 3.0
    return noise * TOKENS ** 0.5 * (top ** columns)[None, None, :]


def block_levels(rng, dims, pieces, least, top_value):
    def one(position, parts):
        heights = jax.random.uniform(jax.random.fold_in(jax.random.fold_in(rng, 6), position), (parts,), jnp.float32, least / len(pieces), top_value / len(pieces))
        return jnp.repeat(jnp.exp(heights), dims[position] // parts).reshape((-1,) + (1,) * (len(dims) - position - 1))

    level = one(*pieces[0])
    for cut in pieces[1:]:
        level = level * one(*cut)
    return level


def gaussian(stream_key, shape, width, reach, pieces=(), kind=jnp.bfloat16):
    drawn = width * jax.random.normal(stream_key, shape, jnp.float32)
    if pieces:
        drawn = drawn * block_levels(stream_key, shape, pieces, -0.22, 0.18)
    return jnp.clip(drawn, -reach, reach).astype(kind)


def setup_inputs(seed: int = 0) -> dict:
    streams_of = jax.random.split(jax.random.key(seed), 11)
    tokens = gaussian(streams_of[0], (TOKENS, D), 1.0, 6.0, ((0, 128),), jnp.float32)
    cotangent = gaussian(streams_of[1], (TOKENS, D), 1.0, 6.0, ((0, 128),), jnp.float32)
    matrices = draw_matrices(jax.random.fold_in(streams_of[10], 71), 0)
    vectors = draw_vectors(jax.random.fold_in(streams_of[10], 71), 0)
    first_moment = gaussian(streams_of[4], (LAYERS, VEC, D), (TOKENS ** 0.5 / 9), 80.0, (), jnp.float32)
    second_moment = jnp.clip(jnp.exp(jax.random.uniform(streams_of[5], (LAYERS, VEC, D), jnp.float32, math.log(862.0), math.log(3276.0))), 862.0, 3276.0)
    momenta = draw_momenta(jax.random.fold_in(streams_of[10], 71), 0)
    lengths = draw_lengths(jax.random.fold_in(streams_of[10], 71), 0)
    assign = draw_assign(jax.random.fold_in(streams_of[10], 71), 0)
    owner_slots = draw_owner_slots(jax.random.fold_in(streams_of[10], 71), 0)
    return {"tokens": tokens, "cotangent": cotangent, "matrices": matrices, "vectors": vectors, "first_moment": first_moment, "second_moment": second_moment, "momenta": momenta, "lengths": lengths, "assign": assign, "owner_slots": owner_slots}


@jax.custom_vjp
def low(v):
    return lax.optimization_barrier(v.astype(jnp.bfloat16)).astype(jnp.float32)

@jax.custom_vjp
def low_back(v):
    return v

def low_keep(v):
    return (low(v), None)

def low_pass(kept, grad):
    return (grad,)

def back_keep(v):
    return (v, None)

def back_low(kept, grad):
    return (low(grad),)
low.defvjp(low_keep, low_pass)
low_back.defvjp(back_keep, back_low)
NORM_EPSILON = 1e-05
MASK_VALUE = -1000000000.0
MUON_DECAY = 0.95
MUON_RATE = 0.5
NS_FIRST = 3.4445
NS_SECOND = -4.775
NS_THIRD = 2.0315
ADAM_FIRST = 0.9
ADAM_SECOND = 0.95
ADAM_EPSILON = 1e-08
VECTOR_RATE = 0.3
NORM_FLOOR = 1e-07
HIGHEST_PRECISION = lax.Precision.HIGHEST

def rounded(values):
    return lax.optimization_barrier(values.astype(jnp.bfloat16)).astype(jnp.float32)

def layer_norm(values, gain, shift):
    center = lax.optimization_barrier(jnp.mean(values, axis=-1, keepdims=True))
    centred = values - center
    spread = lax.optimization_barrier(jnp.mean(centred * centred, axis=-1, keepdims=True))
    return centred * lax.rsqrt(spread + NORM_EPSILON) * gain + shift

def gelu_tanh(values):
    return jax.nn.gelu(values, approximate=True)

def segment_labels(lengths, assign, group, group_rows):
    seq_count = lengths.shape[0]
    member = assign == group
    own_lengths = jnp.where(member, lengths, 0).astype(jnp.int32)
    starts = (jnp.cumsum(own_lengths) - own_lengths).astype(jnp.int32)
    places = lax.iota(jnp.int32, group_rows)
    inside = member[:, None] & (places[None, :] >= starts[:, None]) & (places[None, :] < (starts + own_lengths)[:, None])
    numbers = lax.iota(jnp.int32, seq_count) + 1
    return lax.optimization_barrier(jnp.sum(jnp.where(inside, numbers[:, None], 0), axis=0)).astype(jnp.int32)

def reference_attention(queries, key_rows, value_rows, labels, slopes):
    head_scale = HEAD_DIM ** (-0.5)
    raw = jnp.einsum('qhd,khd->hqk', queries, key_rows, precision=HIGHEST_PRECISION) * head_scale
    places = lax.iota(jnp.int32, queries.shape[0])
    distance = places[:, None] - places[None, :]
    scores = low_back(raw - slopes[:, None, None] * distance.astype(jnp.float32)[None])
    allowed = (labels[:, None] == labels[None, :]) & (distance >= 0)
    scores = jnp.where(allowed[None], scores, MASK_VALUE)
    row_max = lax.optimization_barrier(jnp.max(scores, axis=2, keepdims=True))
    exponent = jnp.exp(scores - row_max)
    probs = low(exponent / lax.optimization_barrier(jnp.sum(exponent, axis=2, keepdims=True)))
    return jnp.einsum('hqk,khd->qhd', probs, value_rows, precision=HIGHEST_PRECISION)

def reference_layer(resid, mats, vecs, labels, slopes):
    blocks = FF // D
    group_rows = resid.shape[0]
    normed_a = low(layer_norm(resid, vecs[0], vecs[1]))
    projected = jnp.einsum('gd,udk->guk', normed_a, mats[0:3], precision=HIGHEST_PRECISION)
    queries = low(low_back(projected[:, 0] + vecs[2]))
    key_rows = low(low_back(projected[:, 1]))
    value_rows = low(low_back(projected[:, 2] + vecs[3]))
    mixed = reference_attention(queries.reshape(group_rows, HEADS, HEAD_DIM), key_rows.reshape(group_rows, HEADS, HEAD_DIM), value_rows.reshape(group_rows, HEADS, HEAD_DIM), labels, slopes)
    attended = low(low_back(mixed.reshape(group_rows, D)))
    middle = resid + low_back(jnp.einsum('gk,ok->go', attended, mats[3], precision=HIGHEST_PRECISION) + vecs[4])
    normed_b = low(layer_norm(middle, vecs[5], vecs[6]))
    pre_act = low_back(jnp.einsum('gd,udk->guk', normed_b, mats[4:4 + blocks], precision=HIGHEST_PRECISION) + vecs[8:8 + blocks][None])
    hidden = low(gelu_tanh(pre_act))
    branch_two = jnp.einsum('guk,uok->go', hidden, mats[4 + blocks:4 + 2 * blocks], precision=HIGHEST_PRECISION)
    return middle + low_back(branch_two + vecs[7])

def group_block(inputs, mats, vecs, labels, slopes):
    for layer_idx in range(LAYERS):
        inputs = reference_layer(inputs, mats[layer_idx], vecs[layer_idx], labels, slopes)
    return inputs

def orthogonal(moment):
    current = moment / (jnp.sqrt(jnp.sum(moment * moment)) + NORM_FLOOR)
    for ns_idx in range(NS_STEPS):
        low_current = rounded(current)
        gram = rounded(jnp.dot(low_current, low_current.T, precision=HIGHEST_PRECISION))
        first_term = jnp.dot(gram, low_current, precision=HIGHEST_PRECISION)
        second_term = jnp.dot(gram, rounded(first_term), precision=HIGHEST_PRECISION)
        current = NS_FIRST * current + NS_SECOND * first_term + NS_THIRD * second_term
    return current

def reference(tokens, cotangent, matrices, vectors, first_moment, second_moment, momenta, lengths, assign, owner_slots):
    group_ids = lax.iota(jnp.int32, N_DP)
    labels = jax.vmap(partial(segment_labels, lengths, assign, group_rows=GROUP))(group_ids)
    slopes = 2.0 ** (-8.0 * (lax.iota(jnp.float32, HEADS) + 1.0) / HEADS)
    checked = jax.checkpoint(group_block)

    def network(mats, vecs, inputs):
        grouped = inputs.reshape(N_DP, GROUP, D)

        def run_group(pair):
            return checked(pair[0], mats, vecs, pair[1], slopes)
        return lax.map(run_group, (grouped, labels)).reshape(TOKENS, D)
    out_tokens, pull = jax.vjp(network, matrices, vectors, tokens)
    valid = (labels.reshape(TOKENS) > 0).astype(jnp.float32)[:, None]
    grad_matrices, grad_vectors, grad_tokens = pull(cotangent * valid)
    new_first = ADAM_FIRST * first_moment + (1.0 - ADAM_FIRST) * grad_vectors
    new_second = ADAM_SECOND * second_moment + (1.0 - ADAM_SECOND) * grad_vectors * grad_vectors
    first_fix = 1.0 - ADAM_FIRST ** STEP
    second_fix = 1.0 - ADAM_SECOND ** STEP
    new_vectors = vectors - VECTOR_RATE * (new_first / first_fix) / (jnp.sqrt(new_second / second_fix) + ADAM_EPSILON)
    unit_grads = grad_matrices.reshape(UNITS, D, D)
    one_hot = (owner_slots[None, :] == lax.iota(jnp.int32, SLOTS)[:, None]).astype(jnp.float32)
    slot_grads = jnp.einsum('su,urc->src', one_hot, unit_grads, precision=HIGHEST_PRECISION)
    new_momenta = MUON_DECAY * momenta + slot_grads
    momentum_scales = jnp.sqrt(lax.optimization_barrier(jnp.sum(new_momenta * new_momenta, axis=(1, 2)))) / (float(TOKENS) ** 0.5 * D)
    slot_steps = lax.map(orthogonal, new_momenta)
    unit_steps = jnp.einsum('su,src->urc', one_hot, slot_steps, precision=HIGHEST_PRECISION)
    new_matrices = matrices - MUON_RATE * unit_steps.reshape(LAYERS, VEC, D, D)
    return (out_tokens, grad_tokens, grad_matrices, new_matrices, new_momenta, grad_vectors, new_first, new_second, new_vectors, momentum_scales)
```

```python
import jax
import jax.numpy as jnp
from jax import lax
from jax.experimental import pallas as pl
from jax.experimental.pallas import tpu as pltpu
from jax.sharding import Mesh
from jax.sharding import PartitionSpec as P

D = 1024
HEADS = 16
FF = 4096
HEAD_DIM = 64
LAYERS = 2
UNITS = 24
NS_STEPS = 5
STEP = 10


NORM_EPSILON = 1e-05
MASK_VALUE = -1000000000.0
MUON_DECAY = 0.95
MUON_RATE = 0.5
NS_FIRST = 3.4445
NS_SECOND = -4.775
NS_THIRD = 2.0315
ADAM_FIRST = 0.9
ADAM_SECOND = 0.95
ADAM_EPSILON = 1e-08
VECTOR_RATE = 0.3
NORM_FLOOR = 1e-07
HIGHEST_PRECISION = lax.Precision.HIGHEST


def layer_norm(values, gain, shift):
    center = jnp.mean(values, axis=-1, keepdims=True)
    centred = values - center
    spread = jnp.mean(centred * centred, axis=-1, keepdims=True)
    return centred * lax.rsqrt(spread + NORM_EPSILON) * gain + shift


def gelu_tanh(values):
    return jax.nn.gelu(values, approximate=True)


def segment_labels(lengths, assign, group, group_rows):
    seq_count = lengths.shape[0]
    member = assign == group
    own_lengths = jnp.where(member, lengths, 0)
    starts = jnp.cumsum(own_lengths) - own_lengths
    places = lax.iota(jnp.int32, group_rows)
    inside = (
        member[:, None]
        & (places[None, :] >= starts[:, None])
        & (places[None, :] < (starts + own_lengths)[:, None])
    )
    numbers = lax.iota(jnp.int32, seq_count) + 1
    return jnp.sum(jnp.where(inside, numbers[:, None], 0), axis=0)


DP = ("z", "y", "core")
ALL = ("z", "y", "core", "x")
RING = 4
VMEM_BYTES = 32 * 1024 * 1024


def greet(peers):
    barrier = pltpu.get_barrier_semaphore()
    for peer in peers:
        pl.semaphore_signal(
            barrier, inc=1, device_id=peer, device_id_type=pl.DeviceIdType.MESH
        )
    pl.semaphore_wait(barrier, len(peers))


def push(src, dst, send_sem, recv_sem, peer):
    return pltpu.make_async_remote_copy(
        src_ref=src,
        dst_ref=dst,
        send_sem=send_sem,
        recv_sem=recv_sem,
        device_id=peer,
        device_id_type=pl.DeviceIdType.MESH,
    )


class Lanes:
    def __init__(self, send_sems, recv_sems):
        self.send_sems = send_sems
        self.recv_sems = recv_sems
        self.used = 0

        self.copies = []

    def push(self, src, dst, peer):
        copy = push(src, dst, self.send_sems.at[self.used], self.recv_sems.at[self.used], peer)
        self.used += 1
        copy.start()
        self.copies.append(copy)
        return copy

    def finish(self):
        for copy in self.copies:
            copy.wait_send()


def weave(*steps):
    steps = list(steps)
    while steps:
        for step in list(steps):
            try:
                next(step)
            except StopIteration:
                steps.remove(step)
        if steps:
            yield


def ring(axis):
    me = lax.axis_index(axis)
    return me, lax.rem(me + 1, RING), lax.rem(me + 3, RING), lax.rem(me + 2, RING)


def shifted(shifts):
    return {
        axis: lax.rem(lax.axis_index(axis) + shift, 2 if axis == "core" else RING)
        for axis, shift in shifts
    }


def beside(*axes):
    steps = {"core": (1,)}
    return [((axis, shift),) for axis in axes for shift in steps.get(axis, (1, 3))]


def all_of(first, second):
    shifts = [(a, b) for a in range(RING) for b in range(2 if second == "core" else RING)]
    return [
        tuple((axis, shift) for axis, shift in ((first, a), (second, b)) if shift)
        for a, b in shifts[1:]
    ]


def ring_gather(axis, lanes, own, part, early=0, late=0):
    me, right, left, far = ring(axis)
    go_right, go_left = {axis: right}, {axis: left}
    to_right = [lanes.push(own(0), part(me, 0), go_right)]
    to_left = [lanes.push(own(1), part(me, 1), go_left)]
    to_right.append(lanes.push(own(1), part(me, 1), go_right))
    to_left.append(lanes.push(own(0), part(me, 0), go_left))
    yield
    for turn in range(early):
        yield
    to_right[0].wait_recv()
    from_left = part(left, 0)
    to_right.append(lanes.push(from_left, from_left, go_right))
    to_left[0].wait_recv()
    from_right = part(right, 1)
    to_left.append(lanes.push(from_right, from_right, go_left))
    yield
    for turn in range(late):
        yield
    for copy in to_right[1:] + to_left[1:]:
        copy.wait_recv()


def ring_fold(axis, lanes, part, relay, mixed, near, store, early=0, late=0):
    me, right, left, far = ring(axis)
    go_right, go_left = {axis: right}, {axis: left}
    far_right = lanes.push(part(far, 0), relay.at[0], go_right)
    far_left = lanes.push(part(far, 1), relay.at[1], go_left)
    near_right = lanes.push(part(right, 1), near.at[0, 1], go_right)
    near_left = lanes.push(part(left, 0), near.at[1, 0], go_left)
    yield
    for turn in range(early):
        yield

    def mix(side, place):
        mixed[side] = (
            relay[side].astype(jnp.float32) + part(place, side)[...].astype(jnp.float32)
        ).astype(mixed.dtype)

    far_right.wait_recv()
    mix(0, right)
    mixed_right = lanes.push(mixed.at[0], near.at[0, 0], go_right)
    far_left.wait_recv()
    mix(1, left)
    mixed_left = lanes.push(mixed.at[1], near.at[1, 1], go_left)
    yield
    for turn in range(late):
        yield
    near_right.wait_recv()
    near_left.wait_recv()
    mixed_right.wait_recv()
    mixed_left.wait_recv()
    for side in (0, 1):
        store(
            side,
            part(me, side)[...].astype(jnp.float32)
            + near[0, side].astype(jnp.float32)
            + near[1, side].astype(jnp.float32),
        )


def direct_gather(axis, lanes, own, slot):
    me = lax.axis_index(axis)
    copies = [
        lanes.push(own, slot(me), {axis: lax.rem(me + shift, RING)}) for shift in (2, 1, 3)
    ]
    yield
    for copy in copies:
        copy.wait_recv()


def direct_fold(axis, lanes, part, near, store):
    me = lax.axis_index(axis)
    copies = []
    for order, shift in enumerate((2, 1, 3)):
        place = lax.rem(me + shift, RING)
        copies.append(lanes.push(part(place), near.at[order], {axis: place}))
    yield
    total = part(me)[...].astype(jnp.float32)
    for order, copy in enumerate(copies):
        copy.wait_recv()
        total = total + near[order].astype(jnp.float32)
    store(total)


def span(start, size):
    return pl.ds(pl.multiple_of(start * size, size), size)


class Spread:
    peers = beside("x")
    early = late = wait = 0
    copies = 6

    def __init__(self, own):
        rows, columns = own.shape
        self.out = jax.ShapeDtypeStruct((RING * rows, columns), own.dtype)
        self.scratch = [pltpu.SemaphoreType.DMA]

    def steps(self, lanes, own_ref, all_ref, keep_sem):
        for turn in range(self.wait):
            yield
        rows = own_ref.shape[0]
        half = rows // 2
        me = lax.axis_index("x")
        keep = pltpu.make_async_copy(own_ref, all_ref.at[span(me, rows), :], keep_sem)
        keep.start()

        def part(place, side):
            return all_ref.at[span(place * 2 + side, half), :]

        yield from ring_gather("x", lanes, lambda side: own_ref.at[pl.ds(side * half, half), :], part, self.early, self.late)
        keep.wait()


class SpreadLater(Spread):
    def __init__(self, own):
        super().__init__(own)
        self.wait = 3


class Fold:
    peers = beside("x")
    early = late = 0
    copies = 6

    def __init__(self, parts):
        rows, columns = parts.shape
        rows //= RING
        half = (rows // 2, columns)
        self.out = jax.ShapeDtypeStruct((rows, columns), jnp.float32)
        self.scratch = [
            pltpu.VMEM((2,) + half, parts.dtype),
            pltpu.VMEM((2,) + half, parts.dtype),
            pltpu.VMEM((2, 2) + half, parts.dtype),
        ]

    def steps(self, lanes, parts_ref, total_ref, relay, mixed, near):
        half = total_ref.shape[0] // 2

        def part(place, side):
            return parts_ref.at[span(place * 2 + side, half), :]

        def store(side, value):
            total_ref[pl.ds(side * half, half), :] = value

        yield from ring_fold(
            "x", lanes, part, relay, mixed, near, store, self.early, self.late
        )


class Gather:
    peers = beside("y", "z", "core") + [(("y", 2),), (("z", 2),)]
    copies = 21
    patience = 0

    def __init__(self, own):
        self.out = jax.ShapeDtypeStruct((4, 4, 2) + own.shape, own.dtype)
        self.scratch = []

    def steps(self, lanes, own_ref, all_ref):
        wide = own_ref.shape[1] // 2
        slim = wide // 2
        z, y, core = (lax.axis_index(name) for name in DP)
        twin = 1 - core
        sibling = {"core": twin}
        mine = span(core, wide)
        swap = lanes.push(own_ref.at[:, span(twin, wide)], all_ref.at[z, y, core, :, span(twin, wide)], sibling)
        all_ref[z, y, core, :, mine] = own_ref[:, mine]

        def flow(row, first):
            def cut(side):
                return span(core * 2 + side, slim)

            def in_y(place):
                return all_ref.at[z, place, row, :, mine]

            def in_z(place):
                return all_ref.at[place, y, row, :, mine]

            def over_z(place, side):
                return all_ref.at[place, :, row, :, cut(side)]

            def over_y(place, side):
                return all_ref.at[:, place, row, :, cut(side)]

            if first == "y":
                yield from direct_gather("y", lanes, in_y(y), in_y)
                yield from ring_gather("z", lanes, lambda side: over_z(z, side), over_z, 0, self.patience)
            else:
                yield from direct_gather("z", lanes, in_z(z), in_z)
                yield from ring_gather("y", lanes, lambda side: over_y(y, side), over_y, 0, self.patience)
            done = all_ref.at[:, :, row, :, mine]
            backs.append(lanes.push(done, done, sibling))

        def own_flow():
            yield from flow(core, "y")

        def twin_flow():
            swap.wait_recv()
            yield from flow(twin, "z")

        backs = []
        yield from weave(own_flow(), twin_flow())
        yield
        for copy in backs:
            copy.wait_recv()


class Share:
    peers = beside("y", "z", "core") + [(("y", 2),), (("z", 2),)]


def times(left, right):
    return lax.dot_general(
        left, right, (((0,), (0,)), ((), ())), preferred_element_type=jnp.float32
    )


class ShareFirst(Share):
    peers = beside("core")
    copies = 2

    def __init__(self, *operands):
        self.spans = [min(array.shape[1], self.block) for array in operands[1::2]]
        rows = operands[0].shape[1] // 32
        wide = sum(array.shape[1] for array in operands[1::2]) // 2
        dtype = operands[0].dtype
        self.out = jax.ShapeDtypeStruct((2, RING, RING, rows, wide), dtype)
        whole = (RING, RING, 2, rows, wide)
        self.scratch = [
            pltpu.VMEM(whole, dtype),
            pltpu.VMEM(whole, dtype),
            pltpu.VMEM(self.out.shape, dtype),
        ]

    def steps(self, lanes, *refs):
        operands, (pair_ref, give_ref, keep_ref, got_ref) = refs[:-4], refs[-4:]
        core = lax.axis_index("core")
        twin = 1 - core
        rows = (twin, core)

        def multiply(half, target):
            def one(place, carry):
                parts = []
                for left, right, size in zip(operands[::2], operands[1::2], self.spans):
                    columns = [
                        right[:, pl.ds(pl.multiple_of(start + half * (size // 2), 128), size // 2)]
                        for start in range(0, right.shape[1], size)
                    ]
                    picked = columns[0] if len(columns) == 1 else jnp.concatenate(columns, axis=1)
                    step = left.shape[1] // RING
                    parts.append(times(left[:, span(place, step)], picked))
                value = jnp.concatenate(parts, axis=1).astype(target.dtype)
                target[place] = value.reshape(target.shape[1:])
                return carry

            lax.fori_loop(0, RING, one, 0)

        multiply(twin, give_ref)
        swaps = [
            lanes.push(give_ref.at[:, :, rows[1 - order]], got_ref.at[order], {"core": twin})
            for order in (0, 1)
        ]
        multiply(core, keep_ref)
        yield
        for order in (0, 1):
            swaps[order].wait_recv()

            def pair_up(place, carry):
                pair_ref[order, place] = (
                    got_ref[order, place].astype(jnp.float32)
                    + keep_ref[place, :, rows[order]].astype(jnp.float32)
                ).astype(pair_ref.dtype)
                return carry

            lax.fori_loop(0, RING, pair_up, 0)


class ShareWhole(ShareFirst):
    peers = Share.peers
    copies = ShareFirst.copies + 12 + 7

    def __init__(self, *operands):
        super().__init__(*operands)
        pair = self.out
        self.second = ShareSecond(pair)
        self.third = ShareThird(self.second.out)
        self.out = self.third.out
        self.scratch = (
            [pltpu.VMEM(pair.shape, pair.dtype)]
            + self.scratch
            + [pltpu.VMEM(self.second.out.shape, pair.dtype)]
            + self.second.scratch
            + self.third.scratch
        )
        self.count = len(operands)

    def steps(self, lanes, *refs):
        operands, own_ref, refs = refs[: self.count], refs[self.count], refs[self.count + 1 :]
        pair_ref, first, refs = refs[0], refs[1:4], refs[4:]
        line_ref, refs = refs[0], refs[1:]
        cut = len(self.second.scratch)
        yield from super().steps(lanes, *operands, pair_ref, *first)
        yield from self.second.steps(lanes, pair_ref, line_ref, *refs[:cut])
        yield from self.third.steps(lanes, line_ref, own_ref, *refs[cut:])


class ShareMlp(ShareWhole):
    block = D


class ShareHeads(ShareWhole):
    block = D // RING


class ShareSecond(Share):
    peers = beside("y", "z")
    copies = 12

    def __init__(self, pair):
        rows, wide = pair.shape[3:]
        big = (RING, rows, wide // 2)
        self.out = jax.ShapeDtypeStruct((2, RING, rows, wide), pair.dtype)
        self.scratch = [
            pltpu.VMEM(lead + big, pair.dtype) for lead in ((2,), (2,), (2, 2)) * 2
        ]

    def steps(self, lanes, pair_ref, line_ref, *buffers):
        slim = line_ref.shape[3] // 2

        def flow(order, axis):
            def part(place, side):
                cut = pl.ds(side * slim, slim)
                if order:
                    return pair_ref.at[order, :, place, :, cut]
                return pair_ref.at[order, place, :, :, cut]

            def store(side, value):
                line_ref[order, :, :, pl.ds(side * slim, slim)] = value.astype(line_ref.dtype)

            yield from ring_fold(axis, lanes, part, *buffers[3 * order : 3 * order + 3], store)

        yield from weave(flow(0, "z"), flow(1, "y"))


class ShareThird(Share):
    copies = 7

    def __init__(self, line):
        rows, wide = line.shape[2:]
        self.out = jax.ShapeDtypeStruct((rows, 2 * wide), line.dtype)
        self.scratch = [
            pltpu.VMEM((2, rows, wide), line.dtype),
            pltpu.VMEM((2, RING - 1, rows, wide), line.dtype),
        ]

    def steps(self, lanes, line_ref, own_ref, last, near):
        core = lax.axis_index("core")
        mine = span(core, own_ref.shape[1] // 2)

        def flow(order, axis):
            def part(place):
                return line_ref.at[order, place]

            def store(value):
                last[order] = value.astype(last.dtype)

            yield from direct_fold(axis, lanes, part, near.at[order], store)

        yield from weave(flow(0, "y"), flow(1, "z"))
        back = lanes.push(last.at[0], own_ref.at[:, mine], {"core": 1 - core})
        own_ref[:, mine] = last[1]
        yield
        back.wait_recv()


DEALT = [
    ((("z", a),) if a else ()) + ((("y", b),) if b else ()) + ((("core", c),) if c else ())
    for a in (0, 1, 3, 2)
    for b in range(RING)
    for c in range(2)
]


def dp_place(shifts):
    at = {axis: lax.axis_index(axis) for axis in DP} | shifted(shifts)
    return (at["z"] * RING + at["y"]) * 2 + at["core"]


class Moments:
    peers = DEALT[1:] + beside("x")
    copies = 31 + 4 * 6

    def __init__(self, outgoing, momenta):
        rows, width = momenta.shape
        self.out = (
            jax.ShapeDtypeStruct(momenta.shape, momenta.dtype),
            jax.ShapeDtypeStruct((rows, RING * width), outgoing.dtype),
        )
        self.scratch = [pltpu.VMEM(outgoing.shape, outgoing.dtype)]

    def steps(self, lanes, outgoing_ref, momenta_ref, new_ref, moment_ref, arrived_ref):
        width = momenta_ref.shape[1]
        rows = momenta_ref.shape[0] // RING
        half = rows // 2
        z, x, mine = lax.axis_index("z"), lax.axis_index("x"), dp_place(())
        copies = [
            lanes.push(outgoing_ref.at[dp_place(peer)], arrived_ref.at[mine], shifted(peer))
            for peer in DEALT[1:]
        ]
        arrived_ref[mine] = outgoing_ref[mine]

        def flow(order, wait, early, late):
            for turn in range(wait):
                yield
            source = lax.rem(z + (0, 3, 1, 2)[order], RING)
            for copy in copies[max(8 * order - 1, 0) : 8 * order + 7]:
                copy.wait_recv()
            place = span(source, rows)
            arrived = arrived_ref[span(source, 8)].astype(jnp.float32).reshape(rows, width)
            value = MUON_DECAY * momenta_ref[place, :] + arrived
            new_ref[place, :] = value
            moment_ref[place, span(x, width)] = value.astype(moment_ref.dtype)

            def part(place, side):
                return moment_ref.at[span(source * 2 + side, half), span(place, width)]

            yield from ring_gather("x", lanes, lambda side: part(x, side), part, early, late)

        yield from weave(
            flow(0, 0, 0, 4), flow(3, 1, 1, 2), flow(1, 0, 1, 3), flow(2, 0, 1, 3)
        )


class Returns:
    peers = DEALT[1:]
    copies = 31

    def __init__(self, steps):
        self.out = jax.ShapeDtypeStruct(steps.shape, steps.dtype)
        self.scratch = []

    def steps(self, lanes, step_ref, back_ref):
        mine = dp_place(())
        copies = [
            lanes.push(step_ref.at[dp_place(peer)], back_ref.at[mine], shifted(peer))
            for peer in DEALT[1:]
        ]
        back_ref[mine] = step_ref[mine]
        yield
        for copy in copies:
            copy.wait_recv()


class Total:
    inner = all_of("x", "core")
    outer = all_of("z", "y")
    peers = inner + outer
    copies = 2 * len(inner) + len(outer)

    def __init__(self, part):
        chunk = part.shape[1:]
        self.out = jax.ShapeDtypeStruct(part.shape, jnp.float32)
        self.scratch = [
            pltpu.VMEM(chunk, jnp.float32),
            pltpu.VMEM((len(self.inner) + 1,) + chunk, jnp.float32),
            pltpu.VMEM((len(self.outer) + 1,) + chunk, jnp.float32),
        ]

    def steps(self, lanes, part_ref, total_ref, own_ref, inner_ref, outer_ref):
        def place(shifts, first, second):
            at = {axis: lax.axis_index(axis) for axis in (first, second)} | shifted(shifts)
            return at[first] * (2 if second == "core" else RING) + at[second]

        def add_up(slots):
            total = slots[0]
            for slot in range(1, slots.shape[0]):
                total = total + slots[slot]
            own_ref[...] = total

        mine = place((), "x", "core")
        copies = [
            lanes.push(part_ref.at[place(peer, "x", "core")], inner_ref.at[mine], shifted(peer))
            for peer in self.inner
        ]
        inner_ref[mine] = part_ref[mine]
        yield
        for copy in copies:
            copy.wait_recv()
        add_up(inner_ref)
        line = place((), "z", "y")
        copies = [lanes.push(own_ref, outer_ref.at[line], shifted(peer)) for peer in self.outer]
        outer_ref[line] = own_ref[...]
        yield
        for copy in copies:
            copy.wait_recv()
        lanes.finish()
        lanes.copies.clear()
        add_up(outer_ref)
        copies = [lanes.push(own_ref, total_ref.at[mine], shifted(peer)) for peer in self.inner]
        total_ref[mine] = own_ref[...]
        yield
        for copy in copies:
            copy.wait_recv()


KERNELS = (
    "attend_first",
    "attend",
    "mlp_first",
    "mlp",
    "mlp_back",
    "mlp_back_first",
    "attend_back",
    "attend_back_first",
    "moments",
    "returns",
)


def ride(name, *pairs, early=0, late=0):
    pairs = [(kind, arrays if isinstance(arrays, tuple) else (arrays,)) for kind, arrays in pairs]
    jobs = [kind(*arrays) for kind, arrays in pairs]
    operands = [array for kind, arrays in pairs for array in arrays]
    results = []
    for job in jobs:
        job.early, job.late = early, late
        job.outs = job.out if isinstance(job.out, tuple) else (job.out,)
        results.extend(job.outs)

    def kernel(*refs):
        ins, refs = list(refs[: len(operands)]), refs[len(operands) :]
        outs, extra = list(refs[: len(results)]), list(refs[len(results) :])
        peers = list(dict.fromkeys(peer for job in jobs for peer in job.peers))
        greet([shifted(peer) for peer in peers])
        steps, every = [], []
        for job, (kind, arrays) in zip(jobs, pairs):
            every.append(Lanes(extra[0], extra[1]))
            own = ins[: len(arrays)] + outs[: len(job.outs)] + extra[2 : 2 + len(job.scratch)]
            steps.append(job.steps(every[-1], *own))
            ins, outs, extra = (
                ins[len(arrays) :],
                outs[len(job.outs) :],
                extra[2 + len(job.scratch) :],
            )
        for turn in weave(*steps):
            pass
        for lanes in every:
            lanes.finish()

    scratch = []
    for job in jobs:
        sems = pltpu.SemaphoreType.DMA((job.copies,))
        scratch += [sems, sems] + job.scratch
    vmem = pl.BlockSpec(memory_space=pltpu.VMEM)
    return pl.pallas_call(
        kernel,
        out_shape=tuple(results),
        in_specs=[vmem] * len(operands),
        out_specs=(vmem,) * len(results),
        scratch_shapes=scratch,
        compiler_params=pltpu.CompilerParams(
            collective_id=KERNELS.index(name), has_side_effects=True, vmem_limit_bytes=VMEM_BYTES
        ),
        name=name,
    )(*operands)


NS_ROWS = 256


def ortho_kernel(moment_ref, step_ref, square_ref, wide_ref, low_ref, gram_ref, poly_ref):
    size = moment_ref.shape[0]
    blocks = size // NS_ROWS

    def block(idx):
        return pl.ds(pl.multiple_of(idx * NS_ROWS, NS_ROWS), NS_ROWS)

    def add_squares(idx, total):
        values = moment_ref[block(idx), :].astype(jnp.float32)
        return total + jnp.sum(values * values, axis=0, keepdims=True)

    squares = lax.fori_loop(0, blocks, add_squares, jnp.zeros((1, size), jnp.float32))
    total = jnp.sum(squares, axis=1, keepdims=True)
    square_ref[...] = jnp.broadcast_to(total, square_ref.shape)
    factor = 1.0 / (jnp.sqrt(total) + NORM_FLOOR)

    @pl.loop(0, blocks)
    def _(idx):
        values = moment_ref[block(idx), :].astype(jnp.float32) * factor
        wide_ref[block(idx), :] = values
        low_ref[block(idx), :] = values.astype(jnp.bfloat16)

    def contract(left, right, dims):
        return lax.dot_general(left, right, (dims, ((), ())), preferred_element_type=jnp.float32)

    def mirror(target_ref, idx, lower):
        start, stop = idx * NS_ROWS, (idx + 1) * NS_ROWS
        target_ref[start:, start:stop] = lower
        if stop < size:
            target_ref[start:stop, stop:] = lower[NS_ROWS:].T

    def make_gram():
        for idx in range(blocks):
            start, stop = idx * NS_ROWS, (idx + 1) * NS_ROWS
            mirror(
                gram_ref,
                idx,
                contract(low_ref[start:, :], low_ref[start:stop, :], ((1,), (1,))).astype(
                    jnp.bfloat16
                ),
            )

    def make_poly():
        make_gram()
        for idx in range(blocks):
            start, stop = idx * NS_ROWS, (idx + 1) * NS_ROWS
            second = contract(gram_ref[start:, :], gram_ref[:, start:stop], ((1,), (0,)))
            own = gram_ref[start:, start:stop].astype(jnp.float32)
            mirror(poly_ref, idx, (NS_SECOND * own + NS_THIRD * second).astype(jnp.bfloat16))

    @pl.loop(0, NS_STEPS - 1)
    def _(step):
        make_poly()
        for idx in range(blocks):
            columns = slice(idx * NS_ROWS, (idx + 1) * NS_ROWS)
            values = NS_FIRST * wide_ref[:, columns] + contract(
                poly_ref[...], low_ref[:, columns], ((1,), (0,))
            )
            wide_ref[:, columns] = values
            low_ref[:, columns] = values.astype(jnp.bfloat16)

    make_gram()
    columns = span(lax.axis_index("x"), step_ref.shape[1])
    first = contract(gram_ref[...], low_ref[:, columns], ((1,), (0,)))
    second = contract(gram_ref[...], first.astype(jnp.bfloat16), ((1,), (0,)))
    step_ref[...] = (
        NS_FIRST * wide_ref[:, columns] + NS_SECOND * first + NS_THIRD * second
    ).astype(jnp.bfloat16)


def orthogonal(moment, width):
    size = moment.shape[0]
    return pl.pallas_call(
        ortho_kernel,
        out_shape=(
            jax.ShapeDtypeStruct((size, width), jnp.bfloat16),
            jax.ShapeDtypeStruct((8, 128), jnp.float32),
        ),
        in_specs=[pl.BlockSpec(memory_space=pltpu.VMEM)],
        out_specs=(
            pl.BlockSpec(memory_space=pltpu.VMEM),
            pl.BlockSpec(memory_space=pltpu.VMEM),
        ),
        scratch_shapes=[
            pltpu.VMEM((size, size), jnp.float32),
            pltpu.VMEM((size, size), jnp.bfloat16),
            pltpu.VMEM((size, size), jnp.bfloat16),
            pltpu.VMEM((size, size), jnp.bfloat16),
        ],
        compiler_params=pltpu.CompilerParams(vmem_limit_bytes=VMEM_BYTES),
        cost_estimate=pl.CostEstimate(
            flops=30 * size**3, bytes_accessed=4 * size * size, transcendentals=0
        ),
        name="ortho",
    )(moment)


def full_weights(gathered):
    return gathered.reshape(D, gathered.shape[-1])


def side_by_side(units):
    return jnp.concatenate(list(units), axis=1)


def split_units(own, blocks):
    pieces = jnp.transpose(own.reshape(own.shape[0], 2, blocks, -1), (2, 1, 0, 3))
    width = pieces.shape[3]
    if width < 256:
        return jnp.concatenate([pieces[:, 0], pieces[:, 1]], axis=2)
    units = pieces.reshape(blocks * 2, own.shape[0], width // 256, 256)
    return jnp.swapaxes(units, 1, 2).reshape(-1, own.shape[0], 256)


def local_slice(row_values, tensor_pos, width):
    return lax.dynamic_slice_in_dim(row_values, tensor_pos * width, width, row_values.ndim - 1)


def spread_local(part_values, tensor_pos):
    width = part_values.shape[-1]
    empty = jnp.zeros(part_values.shape[:-1] + (D,), jnp.float32)
    return lax.dynamic_update_slice_in_dim(
        empty, part_values, tensor_pos * width, part_values.ndim - 1
    )


ATTEND_ROWS = 256


def head_of(values, head):
    return values[:, head * HEAD_DIM : (head + 1) * HEAD_DIM]


def scores_of(queries, key_rows, slope, distance, allowed):
    raw = product(queries, key_rows, 1, 1) * HEAD_DIM ** (-0.5)
    return jnp.where(allowed, raw - slope * distance, MASK_VALUE)


def places_of(start, label_col_ref, label_row_ref):
    if not isinstance(start, int):
        start = pl.multiple_of(start, ATTEND_ROWS)
    rows = pl.ds(start, ATTEND_ROWS)
    shape = (ATTEND_ROWS, label_row_ref.shape[1])
    distance = (
        start
        + lax.broadcasted_iota(jnp.int32, shape, 0)
        - lax.broadcasted_iota(jnp.int32, shape, 1)
    )
    allowed = (label_col_ref[rows, :] == label_row_ref[...]) & (distance >= 0)
    return rows, distance.astype(jnp.float32), allowed


def attend_kernel(
    normed_ref,
    mats_ref,
    bias_ref,
    label_col_ref,
    label_row_ref,
    slope_ref,
    qkv_ref,
    logsum_ref,
    attended_ref,
    partial_ref,
):
    width = attended_ref.shape[1]
    heads = width // HEAD_DIM

    @pl.loop(0, normed_ref.shape[0], step=ATTEND_ROWS)
    def _(start):
        rows = pl.ds(pl.multiple_of(start, ATTEND_ROWS), ATTEND_ROWS)
        qkv_ref[rows, :] = (
            product(normed_ref[rows, :], mats_ref[:, : 3 * width], 1, 0) + bias_ref[...]
        ).astype(jnp.bfloat16)

    @pl.loop(0, normed_ref.shape[0], step=ATTEND_ROWS)
    def _(start):
        rows, distance, allowed = places_of(start, label_col_ref, label_row_ref)
        queries = qkv_ref[rows, :width]
        mixed = []
        for head in range(heads):
            scores = scores_of(
                head_of(queries, head),
                head_of(qkv_ref[:, width : 2 * width], head),
                slope_ref[head : head + 1, :],
                distance,
                allowed,
            )
            row_max = jnp.max(scores, axis=1, keepdims=True)
            exponent = jnp.exp(scores - row_max)
            row_total = jnp.sum(exponent, axis=1, keepdims=True)
            probs = (exponent * (1.0 / row_total)).astype(jnp.bfloat16)
            mixed.append(product(probs, head_of(qkv_ref[:, 2 * width :], head), 1, 0))
            logsum_ref[rows, head : head + 1] = row_max + jnp.log(row_total)
        attended = jnp.concatenate(mixed, axis=1).astype(jnp.bfloat16)
        attended_ref[rows, :] = attended
        partial_ref[rows, :] = product(attended, mats_ref[:, 3 * width :], 1, 1).astype(
            jnp.bfloat16
        )


def attend_back_kernel(
    d_branch_ref,
    mats_ref,
    qkv_ref,
    logsum_ref,
    label_col_ref,
    label_row_ref,
    slope_ref,
    d_qkv_ref,
    partial_ref,
    bias_ref,
    key_acc,
    value_acc,
):
    width = qkv_ref.shape[1] // 3
    heads = width // HEAD_DIM
    scale = HEAD_DIM ** (-0.5)
    key_acc[...] = jnp.zeros_like(key_acc)
    value_acc[...] = jnp.zeros_like(value_acc)

    for start in range(0, qkv_ref.shape[0], ATTEND_ROWS):
        if start:
            yield
        rows, distance, allowed = places_of(start, label_col_ref, label_row_ref)
        d_mixed = product(d_branch_ref[rows, :], mats_ref[:, 3 * width :], 1, 0).astype(
            jnp.bfloat16
        )
        queries = qkv_ref[rows, :width]
        d_queries, d_keys, d_values = [], [], []
        for head in range(heads):
            own_queries = head_of(queries, head)
            key_rows = head_of(qkv_ref[:, width : 2 * width], head)
            scores = scores_of(own_queries, key_rows, slope_ref[head : head + 1, :], distance, allowed)
            probs = jnp.exp(scores - logsum_ref[rows, head : head + 1])
            d_own = head_of(d_mixed, head)
            d_probs = product(d_own, head_of(qkv_ref[:, 2 * width :], head), 1, 1)
            inner = jnp.sum(probs * d_probs, axis=1, keepdims=True)
            d_scores = (probs * (d_probs - inner)).astype(jnp.bfloat16)
            d_queries.append(product(d_scores, key_rows, 1, 0))
            d_keys.append(product(d_scores, own_queries, 0, 0))
            d_values.append(product(probs.astype(jnp.bfloat16), d_own, 0, 0))
        d_qkv_ref[rows, :width] = (jnp.concatenate(d_queries, axis=1) * scale).astype(jnp.bfloat16)
        key_acc[...] += jnp.concatenate(d_keys, axis=1)
        value_acc[...] += jnp.concatenate(d_values, axis=1)

    d_qkv_ref[:, width : 2 * width] = (key_acc[...] * scale).astype(jnp.bfloat16)
    d_qkv_ref[:, 2 * width :] = value_acc[...].astype(jnp.bfloat16)
    bias_ref[...] = jnp.sum(d_qkv_ref[...].astype(jnp.float32), axis=0, keepdims=True)

    @pl.loop(0, qkv_ref.shape[0], step=ATTEND_ROWS)
    def _(start):
        rows = pl.ds(pl.multiple_of(start, ATTEND_ROWS), ATTEND_ROWS)
        partial_ref[rows, :] = product(
            d_qkv_ref[rows, :], mats_ref[:, : 3 * width], 1, 1
        ).astype(jnp.bfloat16)


def product(left, right, left_dim, right_dim):
    return lax.dot_general(
        left, right, (((left_dim,), (right_dim,)), ((), ())), preferred_element_type=jnp.float32
    )


GELU_SCALE = (2.0 / 3.141592653589793) ** 0.5
GELU_CUBE = 0.044715


class Flat:
    def __init__(self, ref):
        self.ref = ref

    def __getitem__(self, key):
        value = self.ref[:, :, :, :, key[1]]
        return value.reshape(-1, value.shape[-1])


class GatherLater(Gather):
    patience = 2


class Sublayer:
    peers = beside("x")
    copies = 12
    spreads = True

    def __init__(self, own, *operands):
        self.count = len(operands)
        group = own.shape[0] * (RING if self.spreads else 1)
        partial = jax.ShapeDtypeStruct((group, own.shape[1]), jnp.bfloat16)
        self.spread, self.fold = Spread(own), Fold(partial)
        self.extra = tuple(
            jax.ShapeDtypeStruct(*shape) for shape in self.results(group, *operands)
        )
        self.own_scratch = self.work(group, *operands)
        self.out = (self.fold.out,) + ((self.spread.out,) if self.spreads else ()) + self.extra
        self.scratch = (
            [pltpu.VMEM(partial.shape, partial.dtype)]
            + (self.spread.scratch if self.spreads else [])
            + self.fold.scratch
            + self.own_scratch
        )

    def work(self, group, *operands):
        return []

    def before(self, lanes, operands, extra, work):
        return []

    def after(self, lanes, rows, operands, extra, work):
        return []

    def steps(self, lanes, own_ref, *refs):
        refs = list(refs)
        operands, refs = refs[: self.count], refs[self.count :]
        total_ref = refs.pop(0)
        rows_ref = refs.pop(0) if self.spreads else own_ref
        extra, refs = refs[: len(self.extra)], refs[len(self.extra) :]
        partial_ref = refs.pop(0)
        keep = [refs.pop(0)] if self.spreads else []
        mixing, work = refs[:3], refs[3:]
        if self.spreads:
            self.spread.early, self.spread.late = self.early, self.late
            yield from weave(
                self.spread.steps(lanes, own_ref, rows_ref, *keep),
                *self.before(lanes, operands, extra, work),
            )
        yield from self.compute(rows_ref, operands, extra, partial_ref, work)
        yield from weave(
            self.fold.steps(lanes, partial_ref, total_ref, *mixing),
            *self.after(lanes, rows_ref, operands, extra, work),
        )


class Attend(Sublayer):
    def results(self, group, mats, bias, *rest):
        width = bias.shape[1] // 3
        return (
            ((group, 3 * width), jnp.bfloat16),
            ((group, width // HEAD_DIM), jnp.float32),
            ((group, width), jnp.bfloat16),
        )

    def compute(self, rows, operands, extra, partial, work):
        attend_kernel(rows, *operands, *extra, partial)
        yield from ()


class AttendFirst(Attend):
    peers = list(dict.fromkeys(Sublayer.peers + Gather.peers))
    copies = Sublayer.copies + Gather.copies

    def results(self, group, shard, bias, *rest):
        self.gather = Gather(shard)
        return super().results(group, shard, bias, *rest) + (
            (self.gather.out.shape, self.gather.out.dtype),
        )

    def before(self, lanes, operands, extra, work):
        return [self.gather.steps(lanes, operands[0], extra[-1])]

    def compute(self, rows, operands, extra, partial, work):
        attend_kernel(rows, Flat(extra[-1]), *operands[1:], *extra[:-1], partial)
        yield from ()


class AttendBack(Sublayer):
    def results(self, group, mats, qkv, *rest):
        return (qkv.shape, jnp.bfloat16), ((1, qkv.shape[1]), jnp.float32)

    def work(self, group, mats, qkv, *rest):
        return [pltpu.VMEM((group, qkv.shape[1] // 3), jnp.float32)] * 2

    def compute(self, rows, operands, extra, partial, work):
        yield from attend_back_kernel(
            rows, *operands[:6], extra[0], partial, extra[1], *work[:2]
        )


class AttendBackFirst(AttendBack):
    peers = list(dict.fromkeys(Sublayer.peers + Share.peers))
    copies = Sublayer.copies + ShareWhole.copies

    def results(self, group, mats, qkv, *rest):
        normed, attended = rest[-2:]
        self.share = ShareHeads(normed, qkv, normed, attended)
        return super().results(group, mats, qkv) + ((self.share.out.shape, self.share.out.dtype),)

    def work(self, group, mats, qkv, *rest):
        return super().work(group, mats, qkv) + self.share.scratch

    def after(self, lanes, rows, operands, extra, work):
        normed, attended = operands[-2:]
        return [self.share.steps(lanes, normed, extra[0], rows, attended, extra[2], *work[2:])]


class Mlp(Sublayer):
    def results(self, group, mats, bias):
        shape = (group, bias.shape[1])
        return (shape, jnp.float32), (shape, jnp.bfloat16)

    def compute(self, rows_ref, operands, extra, partial_ref, work):
        mats_ref, bias_ref = operands
        pre_ref, hidden_ref = extra
        width = bias_ref.shape[1]

        @pl.loop(0, rows_ref.shape[0], step=ATTEND_ROWS)
        def _(start):
            rows = pl.ds(pl.multiple_of(start, ATTEND_ROWS), ATTEND_ROWS)
            pre = product(rows_ref[rows, :], mats_ref[:, :width], 1, 0) + bias_ref[...]
            pre_ref[rows, :] = pre
            bend = jnp.tanh(GELU_SCALE * (pre + GELU_CUBE * pre * pre * pre))
            hidden = (0.5 * pre * (1.0 + bend)).astype(jnp.bfloat16)
            hidden_ref[rows, :] = hidden
            partial_ref[rows, :] = product(hidden, mats_ref[:, width:], 1, 1).astype(jnp.bfloat16)

        yield from ()


class MlpBackFirst(Sublayer):
    def results(self, group, mats, pre):
        return (pre.shape, jnp.bfloat16), ((1, pre.shape[1]), jnp.float32)

    def compute(self, rows_ref, operands, extra, partial_ref, work):
        mats_ref, pre_ref = operands
        d_pre_ref, sums_ref = extra
        width = pre_ref.shape[1]
        sums_ref[...] = jnp.zeros_like(sums_ref)

        @pl.loop(0, rows_ref.shape[0], step=ATTEND_ROWS)
        def _(start):
            rows = pl.ds(pl.multiple_of(start, ATTEND_ROWS), ATTEND_ROWS)
            d_hidden = product(rows_ref[rows, :], mats_ref[:, width:], 1, 0)
            pre = pre_ref[rows, :]
            square = pre * pre
            bend = jnp.tanh(GELU_SCALE * (pre + GELU_CUBE * pre * square))
            slope = 0.5 * (1.0 + bend) + 0.5 * GELU_SCALE * pre * (1.0 - bend * bend) * (
                1.0 + 3.0 * GELU_CUBE * square
            )
            d_pre = (d_hidden * slope).astype(jnp.bfloat16)
            d_pre_ref[rows, :] = d_pre
            sums_ref[...] += jnp.sum(d_pre.astype(jnp.float32), axis=0, keepdims=True)
            partial_ref[rows, :] = product(d_pre, mats_ref[:, :width], 1, 1).astype(jnp.bfloat16)

        yield from ()


class MlpBack(MlpBackFirst):
    spreads = False
    copies = 6


def attend_operands(vec_rows, masks, tensor_pos, width):
    bias_qkv = jnp.concatenate(
        [
            local_slice(vec_rows[2], tensor_pos, width),
            jnp.zeros((width,), jnp.float32),
            local_slice(vec_rows[3], tensor_pos, width),
        ]
    )
    return (bias_qkv[None],) + masks


def low_norm(values, gain, shift):
    return layer_norm(values, gain, shift).astype(jnp.bfloat16)


def mlp_bias(vec_rows, tensor_pos, width):
    return local_slice(vec_rows[8:], tensor_pos, width).reshape(1, -1)


def norm_back(d_normed, values, gain, shift):
    unused, pull = jax.vjp(layer_norm, values, gain, shift)
    return pull(d_normed)


def vector_grads(gains_a, bias_sums, d_branch, gains_b, d_two, up_sums, tensor_pos):
    width = bias_sums.shape[1] // 3
    head_rows = jnp.stack(
        [
            *gains_a,
            spread_local(bias_sums[0, :width], tensor_pos),
            spread_local(bias_sums[0, 2 * width :], tensor_pos),
            jnp.sum(d_branch.astype(jnp.float32), axis=0),
            *gains_b,
            jnp.sum(d_two.astype(jnp.float32), axis=0),
        ]
    )
    return jnp.concatenate([head_rows, spread_local(up_sums.reshape(-1, width), tensor_pos)])


def on_device(
    tokens,
    cotangent,
    matrices,
    vectors,
    first_moment,
    second_moment,
    momenta,
    lengths,
    assign,
    owner_slots,
):
    dp_pos = lax.axis_index(DP)
    tensor_pos = lax.axis_index("x")
    tok_rows = tokens.shape[0]
    group_rows = tok_rows * lax.axis_size("x")
    total_rows = group_rows * lax.axis_size(DP)
    labels = segment_labels(lengths, assign, dp_pos, group_rows)
    own_labels = lax.dynamic_slice_in_dim(labels, tensor_pos * tok_rows, tok_rows)
    width = matrices.shape[3]
    head_count = width // HEAD_DIM
    head_ids = tensor_pos * head_count + lax.iota(jnp.int32, head_count) + 1
    slopes = 2.0 ** (-8.0 * head_ids.astype(jnp.float32) / HEADS)
    low_mats = matrices.astype(jnp.bfloat16)
    grad_rows = cotangent * (own_labels > 0).astype(jnp.float32)[:, None]
    shards = [(side_by_side(layer[:4]), side_by_side(layer[4:])) for layer in low_mats]
    masks = (labels[:, None], labels[None], slopes[:, None])
    first, second = vectors[0], vectors[1]

    heads = attend_operands(first, masks, tensor_pos, width)
    branch, normed_a0, qkv0, logsum0, attended0, mats_a0, mats_m0 = ride(
        "attend_first",
        (AttendFirst, (low_norm(tokens, first[0], first[1]), shards[0][0]) + heads),
        (GatherLater, shards[0][1]),
        late=1,
    )
    mats_a0, mats_m0 = full_weights(mats_a0), full_weights(mats_m0)
    middle0 = tokens + (branch + first[4])
    branch, normed_b0, pre0, hidden0, mats_a1 = ride(
        "mlp_first",
        (Mlp, (low_norm(middle0, first[5], first[6]), mats_m0, mlp_bias(first, tensor_pos, width))),
        (Gather, shards[1][0]),
        late=1,
    )
    mats_a1 = full_weights(mats_a1)
    resid1 = middle0 + (branch + first[7])
    heads = attend_operands(second, masks, tensor_pos, width)
    grad_out = cotangent * (own_labels > 0).astype(jnp.float32)[:, None]
    d_two1 = grad_out.astype(jnp.bfloat16)
    d_two_all1, branch, normed_a1, qkv1, logsum1, attended1, mats_m1 = ride(
        "attend",
        (SpreadLater, d_two1),
        (Attend, (low_norm(resid1, second[0], second[1]), mats_a1) + heads),
        (Gather, shards[1][1]),
        late=1,
    )
    mats_m1 = full_weights(mats_m1)
    middle1 = resid1 + (branch + second[4])
    branch, normed_b1, pre1, hidden1 = ride(
        "mlp",
        (
            Mlp,
            (low_norm(middle1, second[5], second[6]), mats_m1, mlp_bias(second, tensor_pos, width)),
        ),
    )
    resid = middle1 + (branch + second[7])

    d_normed, d_pre1, up_sums1 = ride("mlp_back", (MlpBack, (d_two_all1, mats_m1, pre1)))
    d_norm, *gains_b1 = norm_back(d_normed, middle1, second[5], second[6])
    d_middle1 = grad_out + d_norm
    d_branch1 = d_middle1.astype(jnp.bfloat16)
    d_normed, d_branch_all1, d_qkv1, bias_sums1, own_m1 = ride(
        "attend_back",
        (AttendBack, (d_branch1, mats_a1, qkv1, logsum1) + masks),
        (ShareMlp, (normed_b1, d_pre1, d_two_all1, hidden1)),
    )
    d_norm, *gains_a1 = norm_back(d_normed, resid1, second[0], second[1])
    grad_mid = d_middle1 + d_norm
    d_two0 = grad_mid.astype(jnp.bfloat16)
    d_normed, d_two_all0, d_pre0, up_sums0, own_a1 = ride(
        "mlp_back_first",
        (MlpBackFirst, (d_two0, mats_m0, pre0)),
        (ShareHeads, (normed_a1, d_qkv1, d_branch_all1, attended1)),
    )
    d_norm, *gains_b0 = norm_back(d_normed, middle0, first[5], first[6])
    d_middle0 = grad_mid + d_norm
    d_branch0 = d_middle0.astype(jnp.bfloat16)
    d_normed, d_branch_all0, d_qkv0, bias_sums0, own_a0, own_m0 = ride(
        "attend_back_first",
        (
            AttendBackFirst,
            (d_branch0, mats_a0, qkv0, logsum0) + masks + (normed_a0, attended0),
        ),
        (ShareMlp, (normed_b0, d_pre0, d_two_all0, hidden0)),
    )
    d_norm, *gains_a0 = norm_back(d_normed, tokens, first[0], first[1])
    grad_rows = d_middle0 + d_norm
    vec_first = vector_grads(
        gains_a0, bias_sums0, d_branch0, gains_b0, d_two0, up_sums0, tensor_pos
    )
    vec_second = vector_grads(
        gains_a1, bias_sums1, d_branch1, gains_b1, d_two1, up_sums1, tensor_pos
    )
    own_grads = [own_a0, own_m0, own_a1, own_m1]
    low_grads = jnp.concatenate(
        [split_units(own, blocks) for own, blocks in zip(own_grads, (4, 2, 4, 2))], axis=0
    )
    grad_matrices = low_grads.astype(jnp.float32).reshape(matrices.shape)
    slot_count = momenta.shape[0] * lax.axis_size(DP)
    one_hot = (owner_slots[None, :] == lax.iota(jnp.int32, slot_count)[:, None]).astype(
        jnp.bfloat16
    )
    outgoing = jnp.einsum(
        "su,urc->src", one_hot, low_grads, preferred_element_type=jnp.float32
    ).astype(jnp.bfloat16)
    new_momenta, moment = ride("moments", (Moments, (outgoing, momenta[0])))
    new_momenta = new_momenta[None]
    current, squares = orthogonal(moment, width)
    momentum_scales = jnp.sqrt(squares[0, 0:1]) / (float(total_rows) ** 0.5 * D)
    returned, grad_vectors = ride(
        "returns",
        (Returns, current.reshape(outgoing.shape)),
        (Total, jnp.concatenate([vec_first, vec_second]).reshape(8, 8, 384)),
    )
    grad_vectors = grad_vectors.reshape(vectors.shape)
    new_first = ADAM_FIRST * first_moment + (1.0 - ADAM_FIRST) * grad_vectors
    new_second = ADAM_SECOND * second_moment + (1.0 - ADAM_SECOND) * grad_vectors * grad_vectors
    first_fix = 1.0 - ADAM_FIRST**STEP
    second_fix = 1.0 - ADAM_SECOND**STEP
    new_vectors = vectors - VECTOR_RATE * (new_first / first_fix) / (
        jnp.sqrt(new_second / second_fix) + ADAM_EPSILON
    )
    unit_steps = jnp.einsum("su,src->urc", one_hot, returned, preferred_element_type=jnp.float32)
    new_matrices = matrices - MUON_RATE * unit_steps.reshape(matrices.shape)
    return (
        resid,
        grad_rows,
        grad_matrices,
        new_matrices,
        new_momenta,
        grad_vectors,
        new_first,
        new_second,
        new_vectors,
        momentum_scales,
    )


def solution(mesh):
    fine = Mesh(mesh.devices.reshape(4, 4, 2, RING), ALL)
    rows = P(ALL, None)
    shards = P(None, None, DP, "x")
    slots = P(DP, None, "x")
    return jax.shard_map(
        on_device,
        mesh=fine,
        in_specs=(rows, rows, shards, P(), P(), P(), slots, P(), P(), P()),
        out_specs=(rows, rows, shards, shards, slots, P(), P(), P(), P(), P(DP)),
        check_vma=False,
    )
```

```python
import jax
import jax.numpy as jnp
from jax import lax
from jax.experimental import pallas as pl
from jax.experimental.pallas import tpu as pltpu
from jax.sharding import Mesh
from jax.sharding import PartitionSpec as P

D = 1024
HEADS = 16
FF = 4096
HEAD_DIM = 64
LAYERS = 2
UNITS = 24
NS_STEPS = 5
STEP = 10


NORM_EPSILON = 1e-05
MASK_VALUE = -1000000000.0
MUON_DECAY = 0.95
MUON_RATE = 0.5
NS_FIRST = 3.4445
NS_SECOND = -4.775
NS_THIRD = 2.0315
ADAM_FIRST = 0.9
ADAM_SECOND = 0.95
ADAM_EPSILON = 1e-08
VECTOR_RATE = 0.3
NORM_FLOOR = 1e-07
HIGHEST_PRECISION = lax.Precision.HIGHEST


def layer_norm(values, gain, shift):
    center = jnp.mean(values, axis=-1, keepdims=True)
    centred = values - center
    spread = jnp.mean(centred * centred, axis=-1, keepdims=True)
    return centred * lax.rsqrt(spread + NORM_EPSILON) * gain + shift


def gelu_tanh(values):
    return jax.nn.gelu(values, approximate=True)


def segment_labels(lengths, assign, group, group_rows):
    seq_count = lengths.shape[0]
    member = assign == group
    own_lengths = jnp.where(member, lengths, 0)
    starts = jnp.cumsum(own_lengths) - own_lengths
    places = lax.iota(jnp.int32, group_rows)
    inside = (
        member[:, None]
        & (places[None, :] >= starts[:, None])
        & (places[None, :] < (starts + own_lengths)[:, None])
    )
    numbers = lax.iota(jnp.int32, seq_count) + 1
    return jnp.sum(jnp.where(inside, numbers[:, None], 0), axis=0)


DP = ("z", "y", "core")
ALL = ("z", "y", "core", "x")
RING = 4
VMEM_BYTES = 32 * 1024 * 1024


def greet(peers):
    barrier = pltpu.get_barrier_semaphore()
    for peer in peers:
        pl.semaphore_signal(
            barrier, inc=1, device_id=peer, device_id_type=pl.DeviceIdType.MESH
        )
    pl.semaphore_wait(barrier, len(peers))


def push(src, dst, send_sem, recv_sem, peer):
    return pltpu.make_async_remote_copy(
        src_ref=src,
        dst_ref=dst,
        send_sem=send_sem,
        recv_sem=recv_sem,
        device_id=peer,
        device_id_type=pl.DeviceIdType.MESH,
    )


class Lanes:
    def __init__(self, send_sems, recv_sems):
        self.send_sems = send_sems
        self.recv_sems = recv_sems
        self.used = 0

        self.copies = []

    def push(self, src, dst, peer):
        copy = push(src, dst, self.send_sems.at[self.used], self.recv_sems.at[self.used], peer)
        self.used += 1
        copy.start()
        self.copies.append(copy)
        return copy

    def finish(self):
        for copy in self.copies:
            copy.wait_send()


def weave(*steps):
    steps = list(steps)
    while steps:
        for step in list(steps):
            try:
                next(step)
            except StopIteration:
                steps.remove(step)
        if steps:
            yield


def ring(axis):
    me = lax.axis_index(axis)
    return me, lax.rem(me + 1, RING), lax.rem(me + 3, RING), lax.rem(me + 2, RING)


def shifted(shifts):
    return {
        axis: lax.rem(lax.axis_index(axis) + shift, 2 if axis == "core" else RING)
        for axis, shift in shifts
    }


def beside(*axes):
    steps = {"core": (1,)}
    return [((axis, shift),) for axis in axes for shift in steps.get(axis, (1, 3))]


def all_of(first, second):
    shifts = [(a, b) for a in range(RING) for b in range(2 if second == "core" else RING)]
    return [
        tuple((axis, shift) for axis, shift in ((first, a), (second, b)) if shift)
        for a, b in shifts[1:]
    ]


def ring_gather(axis, lanes, own, part, early=0, late=0):
    me, right, left, far = ring(axis)
    go_right, go_left = {axis: right}, {axis: left}
    to_right = [lanes.push(own(0), part(me, 0), go_right)]
    to_left = [lanes.push(own(1), part(me, 1), go_left)]
    to_right.append(lanes.push(own(1), part(me, 1), go_right))
    to_left.append(lanes.push(own(0), part(me, 0), go_left))
    yield
    for turn in range(early):
        yield
    to_right[0].wait_recv()
    from_left = part(left, 0)
    to_right.append(lanes.push(from_left, from_left, go_right))
    to_left[0].wait_recv()
    from_right = part(right, 1)
    to_left.append(lanes.push(from_right, from_right, go_left))
    yield
    for turn in range(late):
        yield
    for copy in to_right[1:] + to_left[1:]:
        copy.wait_recv()


def ring_fold(axis, lanes, part, relay, mixed, near, store, early=0, late=0):
    me, right, left, far = ring(axis)
    go_right, go_left = {axis: right}, {axis: left}
    far_right = lanes.push(part(far, 0), relay.at[0], go_right)
    far_left = lanes.push(part(far, 1), relay.at[1], go_left)
    near_right = lanes.push(part(right, 1), near.at[0, 1], go_right)
    near_left = lanes.push(part(left, 0), near.at[1, 0], go_left)
    yield
    for turn in range(early):
        yield

    def mix(side, place):
        mixed[side] = (
            relay[side].astype(jnp.float32) + part(place, side)[...].astype(jnp.float32)
        ).astype(mixed.dtype)

    far_right.wait_recv()
    mix(0, right)
    mixed_right = lanes.push(mixed.at[0], near.at[0, 0], go_right)
    far_left.wait_recv()
    mix(1, left)
    mixed_left = lanes.push(mixed.at[1], near.at[1, 1], go_left)
    yield
    for turn in range(late):
        yield
    near_right.wait_recv()
    near_left.wait_recv()
    mixed_right.wait_recv()
    mixed_left.wait_recv()
    for side in (0, 1):
        store(
            side,
            part(me, side)[...].astype(jnp.float32)
            + near[0, side].astype(jnp.float32)
            + near[1, side].astype(jnp.float32),
        )


def direct_gather(axis, lanes, own, slot):
    me = lax.axis_index(axis)
    copies = [
        lanes.push(own, slot(me), {axis: lax.rem(me + shift, RING)}) for shift in (2, 1, 3)
    ]
    yield
    for copy in copies:
        copy.wait_recv()


def direct_fold(axis, lanes, part, near, store):
    me = lax.axis_index(axis)
    copies = []
    for order, shift in enumerate((2, 1, 3)):
        place = lax.rem(me + shift, RING)
        copies.append(lanes.push(part(place), near.at[order], {axis: place}))
    yield
    total = part(me)[...].astype(jnp.float32)
    for order, copy in enumerate(copies):
        copy.wait_recv()
        total = total + near[order].astype(jnp.float32)
    store(total)


def span(start, size):
    return pl.ds(pl.multiple_of(start * size, size), size)


class Spread:
    peers = beside("x")
    early = late = wait = 0
    copies = 6

    def __init__(self, own):
        rows, columns = own.shape
        self.out = jax.ShapeDtypeStruct((RING * rows, columns), own.dtype)
        self.scratch = [pltpu.SemaphoreType.DMA]

    def steps(self, lanes, own_ref, all_ref, keep_sem):
        for turn in range(self.wait):
            yield
        rows = own_ref.shape[0]
        half = rows // 2
        me = lax.axis_index("x")
        keep = pltpu.make_async_copy(own_ref, all_ref.at[span(me, rows), :], keep_sem)
        keep.start()

        def part(place, side):
            return all_ref.at[span(place * 2 + side, half), :]

        yield from ring_gather("x", lanes, lambda side: own_ref.at[pl.ds(side * half, half), :], part, self.early, self.late)
        keep.wait()


class SpreadLater(Spread):
    def __init__(self, own):
        super().__init__(own)
        self.wait = 3


class Fold:
    peers = beside("x")
    early = late = 0
    copies = 6

    def __init__(self, parts):
        rows, columns = parts.shape
        rows //= RING
        half = (rows // 2, columns)
        self.out = jax.ShapeDtypeStruct((rows, columns), jnp.float32)
        self.scratch = [
            pltpu.VMEM((2,) + half, parts.dtype),
            pltpu.VMEM((2,) + half, parts.dtype),
            pltpu.VMEM((2, 2) + half, parts.dtype),
        ]

    def steps(self, lanes, parts_ref, total_ref, relay, mixed, near):
        half = total_ref.shape[0] // 2

        def part(place, side):
            return parts_ref.at[span(place * 2 + side, half), :]

        def store(side, value):
            total_ref[pl.ds(side * half, half), :] = value

        yield from ring_fold(
            "x", lanes, part, relay, mixed, near, store, self.early, self.late
        )


class Gather:
    peers = beside("y", "z", "core") + [(("y", 2),), (("z", 2),)]
    copies = 21
    patience = 0

    def __init__(self, own):
        self.out = jax.ShapeDtypeStruct((4, 4, 2) + own.shape, own.dtype)
        self.scratch = []

    def steps(self, lanes, own_ref, all_ref):
        wide = own_ref.shape[1] // 2
        slim = wide // 2
        z, y, core = (lax.axis_index(name) for name in DP)
        twin = 1 - core
        sibling = {"core": twin}
        mine = span(core, wide)
        swap = lanes.push(own_ref.at[:, span(twin, wide)], all_ref.at[z, y, core, :, span(twin, wide)], sibling)
        all_ref[z, y, core, :, mine] = own_ref[:, mine]

        def flow(row, first):
            def cut(side):
                return span(core * 2 + side, slim)

            def in_y(place):
                return all_ref.at[z, place, row, :, mine]

            def in_z(place):
                return all_ref.at[place, y, row, :, mine]

            def over_z(place, side):
                return all_ref.at[place, :, row, :, cut(side)]

            def over_y(place, side):
                return all_ref.at[:, place, row, :, cut(side)]

            if first == "y":
                yield from direct_gather("y", lanes, in_y(y), in_y)
                yield from ring_gather("z", lanes, lambda side: over_z(z, side), over_z, 0, self.patience)
            else:
                yield from direct_gather("z", lanes, in_z(z), in_z)
                yield from ring_gather("y", lanes, lambda side: over_y(y, side), over_y, 0, self.patience)
            done = all_ref.at[:, :, row, :, mine]
            backs.append(lanes.push(done, done, sibling))

        def own_flow():
            yield from flow(core, "y")

        def twin_flow():
            swap.wait_recv()
            yield from flow(twin, "z")

        backs = []
        yield from weave(own_flow(), twin_flow())
        yield
        for copy in backs:
            copy.wait_recv()


class Share:
    peers = beside("y", "z", "core") + [(("y", 2),), (("z", 2),)]


def times(left, right):
    return lax.dot_general(
        left, right, (((0,), (0,)), ((), ())), preferred_element_type=jnp.float32
    )


class ShareFirst(Share):
    peers = beside("core")
    copies = 2

    def __init__(self, *operands):
        self.spans = [min(array.shape[1], self.block) for array in operands[1::2]]
        rows = operands[0].shape[1] // 32
        wide = sum(array.shape[1] for array in operands[1::2]) // 2
        dtype = operands[0].dtype
        self.out = jax.ShapeDtypeStruct((2, RING, RING, rows, wide), dtype)
        whole = (RING, RING, 2, rows, wide)
        self.scratch = [
            pltpu.VMEM(whole, dtype),
            pltpu.VMEM(whole, dtype),
            pltpu.VMEM(self.out.shape, dtype),
        ]

    def steps(self, lanes, *refs):
        operands, (pair_ref, give_ref, keep_ref, got_ref) = refs[:-4], refs[-4:]
        core = lax.axis_index("core")
        twin = 1 - core
        rows = (twin, core)

        def multiply(half, target):
            def one(place, carry):
                parts = []
                for left, right, size in zip(operands[::2], operands[1::2], self.spans):
                    columns = [
                        right[:, pl.ds(pl.multiple_of(start + half * (size // 2), 128), size // 2)]
                        for start in range(0, right.shape[1], size)
                    ]
                    picked = columns[0] if len(columns) == 1 else jnp.concatenate(columns, axis=1)
                    step = left.shape[1] // RING
                    parts.append(times(left[:, span(place, step)], picked))
                value = jnp.concatenate(parts, axis=1).astype(target.dtype)
                target[place] = value.reshape(target.shape[1:])
                return carry

            lax.fori_loop(0, RING, one, 0)

        multiply(twin, give_ref)
        swaps = [
            lanes.push(give_ref.at[:, :, rows[1 - order]], got_ref.at[order], {"core": twin})
            for order in (0, 1)
        ]
        multiply(core, keep_ref)
        yield
        for order in (0, 1):
            swaps[order].wait_recv()

            def pair_up(place, carry):
                pair_ref[order, place] = (
                    got_ref[order, place].astype(jnp.float32)
                    + keep_ref[place, :, rows[order]].astype(jnp.float32)
                ).astype(pair_ref.dtype)
                return carry

            lax.fori_loop(0, RING, pair_up, 0)


class ShareWhole(ShareFirst):
    peers = Share.peers
    copies = ShareFirst.copies + 12 + 7

    def __init__(self, *operands):
        super().__init__(*operands)
        pair = self.out
        self.second = ShareSecond(pair)
        self.third = ShareThird(self.second.out)
        self.out = self.third.out
        self.scratch = (
            [pltpu.VMEM(pair.shape, pair.dtype)]
            + self.scratch
            + [pltpu.VMEM(self.second.out.shape, pair.dtype)]
            + self.second.scratch
            + self.third.scratch
        )
        self.count = len(operands)

    def steps(self, lanes, *refs):
        operands, own_ref, refs = refs[: self.count], refs[self.count], refs[self.count + 1 :]
        pair_ref, first, refs = refs[0], refs[1:4], refs[4:]
        line_ref, refs = refs[0], refs[1:]
        cut = len(self.second.scratch)
        yield from super().steps(lanes, *operands, pair_ref, *first)
        yield from self.second.steps(lanes, pair_ref, line_ref, *refs[:cut])
        yield from self.third.steps(lanes, line_ref, own_ref, *refs[cut:])


class ShareMlp(ShareWhole):
    block = D


class ShareHeads(ShareWhole):
    block = D // RING


class ShareSecond(Share):
    peers = beside("y", "z")
    copies = 12

    def __init__(self, pair):
        rows, wide = pair.shape[3:]
        big = (RING, rows, wide // 2)
        self.out = jax.ShapeDtypeStruct((2, RING, rows, wide), pair.dtype)
        self.scratch = [
            pltpu.VMEM(lead + big, pair.dtype) for lead in ((2,), (2,), (2, 2)) * 2
        ]

    def steps(self, lanes, pair_ref, line_ref, *buffers):
        slim = line_ref.shape[3] // 2

        def flow(order, axis):
            def part(place, side):
                cut = pl.ds(side * slim, slim)
                if order:
                    return pair_ref.at[order, :, place, :, cut]
                return pair_ref.at[order, place, :, :, cut]

            def store(side, value):
                line_ref[order, :, :, pl.ds(side * slim, slim)] = value.astype(line_ref.dtype)

            yield from ring_fold(axis, lanes, part, *buffers[3 * order : 3 * order + 3], store)

        yield from weave(flow(0, "z"), flow(1, "y"))


class ShareThird(Share):
    copies = 7

    def __init__(self, line):
        rows, wide = line.shape[2:]
        self.out = jax.ShapeDtypeStruct((rows, 2 * wide), line.dtype)
        self.scratch = [
            pltpu.VMEM((2, rows, wide), line.dtype),
            pltpu.VMEM((2, RING - 1, rows, wide), line.dtype),
        ]

    def steps(self, lanes, line_ref, own_ref, last, near):
        core = lax.axis_index("core")
        mine = span(core, own_ref.shape[1] // 2)

        def flow(order, axis):
            def part(place):
                return line_ref.at[order, place]

            def store(value):
                last[order] = value.astype(last.dtype)

            yield from direct_fold(axis, lanes, part, near.at[order], store)

        yield from weave(flow(0, "y"), flow(1, "z"))
        back = lanes.push(last.at[0], own_ref.at[:, mine], {"core": 1 - core})
        own_ref[:, mine] = last[1]
        yield
        back.wait_recv()


DEALT = [
    ((("z", a),) if a else ()) + ((("y", b),) if b else ()) + ((("core", c),) if c else ())
    for a in (0, 1, 3, 2)
    for b in range(RING)
    for c in range(2)
]


def dp_place(shifts):
    at = {axis: lax.axis_index(axis) for axis in DP} | shifted(shifts)
    return (at["z"] * RING + at["y"]) * 2 + at["core"]


class Moments:
    peers = DEALT[1:] + beside("x")
    copies = 31 + 4 * 6

    def __init__(self, outgoing, momenta):
        rows, width = momenta.shape
        self.out = (
            jax.ShapeDtypeStruct(momenta.shape, momenta.dtype),
            jax.ShapeDtypeStruct((rows, RING * width), outgoing.dtype),
        )
        self.scratch = [pltpu.VMEM(outgoing.shape, outgoing.dtype)]

    def steps(self, lanes, outgoing_ref, momenta_ref, new_ref, moment_ref, arrived_ref):
        width = momenta_ref.shape[1]
        rows = momenta_ref.shape[0] // RING
        half = rows // 2
        z, x, mine = lax.axis_index("z"), lax.axis_index("x"), dp_place(())
        copies = [
            lanes.push(outgoing_ref.at[dp_place(peer)], arrived_ref.at[mine], shifted(peer))
            for peer in DEALT[1:]
        ]
        arrived_ref[mine] = outgoing_ref[mine]

        def flow(order, wait, early, late):
            for turn in range(wait):
                yield
            source = lax.rem(z + (0, 3, 1, 2)[order], RING)
            for copy in copies[max(8 * order - 1, 0) : 8 * order + 7]:
                copy.wait_recv()
            place = span(source, rows)
            arrived = arrived_ref[span(source, 8)].astype(jnp.float32).reshape(rows, width)
            value = MUON_DECAY * momenta_ref[place, :] + arrived
            new_ref[place, :] = value
            moment_ref[place, span(x, width)] = value.astype(moment_ref.dtype)

            def part(place, side):
                return moment_ref.at[span(source * 2 + side, half), span(place, width)]

            yield from ring_gather("x", lanes, lambda side: part(x, side), part, early, late)

        yield from weave(
            flow(0, 0, 0, 4), flow(3, 1, 1, 2), flow(1, 0, 1, 3), flow(2, 0, 1, 3)
        )


class Returns:
    peers = DEALT[1:]
    copies = 31

    def __init__(self, steps):
        self.out = jax.ShapeDtypeStruct(steps.shape, steps.dtype)
        self.scratch = []

    def steps(self, lanes, step_ref, back_ref):
        mine = dp_place(())
        copies = [
            lanes.push(step_ref.at[dp_place(peer)], back_ref.at[mine], shifted(peer))
            for peer in DEALT[1:]
        ]
        back_ref[mine] = step_ref[mine]
        yield
        for copy in copies:
            copy.wait_recv()


class Total:
    inner = all_of("x", "core")
    outer = all_of("z", "y")
    peers = inner + outer
    copies = 2 * len(inner) + len(outer)

    def __init__(self, part):
        chunk = part.shape[1:]
        self.out = jax.ShapeDtypeStruct(part.shape, jnp.float32)
        self.scratch = [
            pltpu.VMEM(chunk, jnp.float32),
            pltpu.VMEM((len(self.inner) + 1,) + chunk, jnp.float32),
            pltpu.VMEM((len(self.outer) + 1,) + chunk, jnp.float32),
        ]

    def steps(self, lanes, part_ref, total_ref, own_ref, inner_ref, outer_ref):
        def place(shifts, first, second):
            at = {axis: lax.axis_index(axis) for axis in (first, second)} | shifted(shifts)
            return at[first] * (2 if second == "core" else RING) + at[second]

        def add_up(slots):
            total = slots[0]
            for slot in range(1, slots.shape[0]):
                total = total + slots[slot]
            own_ref[...] = total

        mine = place((), "x", "core")
        copies = [
            lanes.push(part_ref.at[place(peer, "x", "core")], inner_ref.at[mine], shifted(peer))
            for peer in self.inner
        ]
        inner_ref[mine] = part_ref[mine]
        yield
        for copy in copies:
            copy.wait_recv()
        add_up(inner_ref)
        line = place((), "z", "y")
        copies = [lanes.push(own_ref, outer_ref.at[line], shifted(peer)) for peer in self.outer]
        outer_ref[line] = own_ref[...]
        yield
        yield
        for copy in copies:
            copy.wait_recv()
        lanes.finish()
        lanes.copies.clear()
        add_up(outer_ref)
        copies = [lanes.push(own_ref, total_ref.at[mine], shifted(peer)) for peer in self.inner]
        total_ref[mine] = own_ref[...]
        yield
        for copy in copies:
            copy.wait_recv()


KERNELS = (
    "attend_first",
    "attend",
    "mlp_first",
    "mlp",
    "mlp_back",
    "mlp_back_first",
    "attend_back",
    "attend_back_first",
    "moments",
    "returns",
)


def ride(name, *pairs, early=0, late=0):
    pairs = [(kind, arrays if isinstance(arrays, tuple) else (arrays,)) for kind, arrays in pairs]
    jobs = [kind(*arrays) for kind, arrays in pairs]
    operands = [array for kind, arrays in pairs for array in arrays]
    results = []
    for job in jobs:
        job.early, job.late = early, late
        job.outs = job.out if isinstance(job.out, tuple) else (job.out,)
        results.extend(job.outs)

    def kernel(*refs):
        ins, refs = list(refs[: len(operands)]), refs[len(operands) :]
        outs, extra = list(refs[: len(results)]), list(refs[len(results) :])
        peers = list(dict.fromkeys(peer for job in jobs for peer in job.peers))
        greet([shifted(peer) for peer in peers])
        steps, every = [], []
        for job, (kind, arrays) in zip(jobs, pairs):
            every.append(Lanes(extra[0], extra[1]))
            own = ins[: len(arrays)] + outs[: len(job.outs)] + extra[2 : 2 + len(job.scratch)]
            steps.append(job.steps(every[-1], *own))
            ins, outs, extra = (
                ins[len(arrays) :],
                outs[len(job.outs) :],
                extra[2 + len(job.scratch) :],
            )
        for turn in weave(*steps):
            pass
        for lanes in every:
            lanes.finish()

    scratch = []
    for job in jobs:
        sems = pltpu.SemaphoreType.DMA((job.copies,))
        scratch += [sems, sems] + job.scratch
    vmem = pl.BlockSpec(memory_space=pltpu.VMEM)
    return pl.pallas_call(
        kernel,
        out_shape=tuple(results),
        in_specs=[vmem] * len(operands),
        out_specs=(vmem,) * len(results),
        scratch_shapes=scratch,
        compiler_params=pltpu.CompilerParams(
            collective_id=KERNELS.index(name), has_side_effects=True, vmem_limit_bytes=VMEM_BYTES
        ),
        name=name,
    )(*operands)


NS_ROWS = 256


def ortho_kernel(moment_ref, step_ref, square_ref, wide_ref, low_ref, gram_ref, poly_ref):
    size = moment_ref.shape[0]
    blocks = size // NS_ROWS

    def block(idx):
        return pl.ds(pl.multiple_of(idx * NS_ROWS, NS_ROWS), NS_ROWS)

    def add_squares(idx, total):
        values = moment_ref[block(idx), :].astype(jnp.float32)
        return total + jnp.sum(values * values, axis=0, keepdims=True)

    squares = lax.fori_loop(0, blocks, add_squares, jnp.zeros((1, size), jnp.float32))
    total = jnp.sum(squares, axis=1, keepdims=True)
    square_ref[...] = jnp.broadcast_to(total, square_ref.shape)
    factor = 1.0 / (jnp.sqrt(total) + NORM_FLOOR)

    @pl.loop(0, blocks)
    def _(idx):
        values = moment_ref[block(idx), :].astype(jnp.float32) * factor
        wide_ref[block(idx), :] = values
        low_ref[block(idx), :] = values.astype(jnp.bfloat16)

    def contract(left, right, dims):
        return lax.dot_general(left, right, (dims, ((), ())), preferred_element_type=jnp.float32)

    def mirror(target_ref, idx, lower):
        start, stop = idx * NS_ROWS, (idx + 1) * NS_ROWS
        target_ref[start:, start:stop] = lower
        if stop < size:
            target_ref[start:stop, stop:] = lower[NS_ROWS:].T

    def make_gram():
        for idx in range(blocks):
            start, stop = idx * NS_ROWS, (idx + 1) * NS_ROWS
            mirror(
                gram_ref,
                idx,
                contract(low_ref[start:, :], low_ref[start:stop, :], ((1,), (1,))).astype(
                    jnp.bfloat16
                ),
            )

    def make_poly():
        make_gram()
        for idx in range(blocks):
            start, stop = idx * NS_ROWS, (idx + 1) * NS_ROWS
            second = contract(gram_ref[start:, :], gram_ref[:, start:stop], ((1,), (0,)))
            own = gram_ref[start:, start:stop].astype(jnp.float32)
            mirror(poly_ref, idx, (NS_SECOND * own + NS_THIRD * second).astype(jnp.bfloat16))

    @pl.loop(0, NS_STEPS - 1)
    def _(step):
        make_poly()
        for idx in range(blocks):
            columns = slice(idx * NS_ROWS, (idx + 1) * NS_ROWS)
            values = NS_FIRST * wide_ref[:, columns] + contract(
                poly_ref[...], low_ref[:, columns], ((1,), (0,))
            )
            wide_ref[:, columns] = values
            low_ref[:, columns] = values.astype(jnp.bfloat16)

    make_gram()
    columns = span(lax.axis_index("x"), step_ref.shape[1])
    first = contract(gram_ref[...], low_ref[:, columns], ((1,), (0,)))
    second = contract(gram_ref[...], first.astype(jnp.bfloat16), ((1,), (0,)))
    step_ref[...] = (
        NS_FIRST * wide_ref[:, columns] + NS_SECOND * first + NS_THIRD * second
    ).astype(jnp.bfloat16)


def orthogonal(moment, width):
    size = moment.shape[0]
    return pl.pallas_call(
        ortho_kernel,
        out_shape=(
            jax.ShapeDtypeStruct((size, width), jnp.bfloat16),
            jax.ShapeDtypeStruct((8, 128), jnp.float32),
        ),
        in_specs=[pl.BlockSpec(memory_space=pltpu.VMEM)],
        out_specs=(
            pl.BlockSpec(memory_space=pltpu.VMEM),
            pl.BlockSpec(memory_space=pltpu.VMEM),
        ),
        scratch_shapes=[
            pltpu.VMEM((size, size), jnp.float32),
            pltpu.VMEM((size, size), jnp.bfloat16),
            pltpu.VMEM((size, size), jnp.bfloat16),
            pltpu.VMEM((size, size), jnp.bfloat16),
        ],
        compiler_params=pltpu.CompilerParams(vmem_limit_bytes=VMEM_BYTES),
        cost_estimate=pl.CostEstimate(
            flops=30 * size**3, bytes_accessed=4 * size * size, transcendentals=0
        ),
        name="ortho",
    )(moment)


def full_weights(gathered):
    return gathered.reshape(D, gathered.shape[-1])


def side_by_side(units):
    return jnp.concatenate(list(units), axis=1)


def split_units(own, blocks):
    pieces = jnp.transpose(own.reshape(own.shape[0], 2, blocks, -1), (2, 1, 0, 3))
    width = pieces.shape[3]
    if width < 256:
        return jnp.concatenate([pieces[:, 0], pieces[:, 1]], axis=2)
    units = pieces.reshape(blocks * 2, own.shape[0], width // 256, 256)
    return jnp.swapaxes(units, 1, 2).reshape(-1, own.shape[0], 256)


def local_slice(row_values, tensor_pos, width):
    return lax.dynamic_slice_in_dim(row_values, tensor_pos * width, width, row_values.ndim - 1)


def spread_local(part_values, tensor_pos):
    width = part_values.shape[-1]
    empty = jnp.zeros(part_values.shape[:-1] + (D,), jnp.float32)
    return lax.dynamic_update_slice_in_dim(
        empty, part_values, tensor_pos * width, part_values.ndim - 1
    )


ATTEND_ROWS = 256


def head_of(values, head):
    return values[:, head * HEAD_DIM : (head + 1) * HEAD_DIM]


def scores_of(queries, key_rows, slope, distance, allowed):
    raw = product(queries, key_rows, 1, 1) * HEAD_DIM ** (-0.5)
    return jnp.where(allowed, raw - slope * distance, MASK_VALUE)


def places_of(start, label_col_ref, label_row_ref):
    if not isinstance(start, int):
        start = pl.multiple_of(start, ATTEND_ROWS)
    rows = pl.ds(start, ATTEND_ROWS)
    shape = (ATTEND_ROWS, label_row_ref.shape[1])
    distance = (
        start
        + lax.broadcasted_iota(jnp.int32, shape, 0)
        - lax.broadcasted_iota(jnp.int32, shape, 1)
    )
    allowed = (label_col_ref[rows, :] == label_row_ref[...]) & (distance >= 0)
    return rows, distance.astype(jnp.float32), allowed


def attend_kernel(
    normed_ref,
    mats_ref,
    bias_ref,
    label_col_ref,
    label_row_ref,
    slope_ref,
    qkv_ref,
    logsum_ref,
    attended_ref,
    partial_ref,
):
    width = attended_ref.shape[1]
    heads = width // HEAD_DIM

    @pl.loop(0, normed_ref.shape[0], step=ATTEND_ROWS)
    def _(start):
        rows = pl.ds(pl.multiple_of(start, ATTEND_ROWS), ATTEND_ROWS)
        qkv_ref[rows, :] = (
            product(normed_ref[rows, :], mats_ref[:, : 3 * width], 1, 0) + bias_ref[...]
        ).astype(jnp.bfloat16)

    @pl.loop(0, normed_ref.shape[0], step=ATTEND_ROWS)
    def _(start):
        rows, distance, allowed = places_of(start, label_col_ref, label_row_ref)
        queries = qkv_ref[rows, :width]
        mixed = []
        for head in range(heads):
            scores = scores_of(
                head_of(queries, head),
                head_of(qkv_ref[:, width : 2 * width], head),
                slope_ref[head : head + 1, :],
                distance,
                allowed,
            )
            row_max = jnp.max(scores, axis=1, keepdims=True)
            exponent = jnp.exp(scores - row_max)
            row_total = jnp.sum(exponent, axis=1, keepdims=True)
            probs = (exponent * (1.0 / row_total)).astype(jnp.bfloat16)
            mixed.append(product(probs, head_of(qkv_ref[:, 2 * width :], head), 1, 0))
            logsum_ref[rows, head : head + 1] = row_max + jnp.log(row_total)
        attended = jnp.concatenate(mixed, axis=1).astype(jnp.bfloat16)
        attended_ref[rows, :] = attended
        partial_ref[rows, :] = product(attended, mats_ref[:, 3 * width :], 1, 1).astype(
            jnp.bfloat16
        )


def attend_back_kernel(
    d_branch_ref,
    mats_ref,
    qkv_ref,
    logsum_ref,
    label_col_ref,
    label_row_ref,
    slope_ref,
    d_qkv_ref,
    bias_ref,
    key_acc,
    value_acc,
):
    width = qkv_ref.shape[1] // 3
    heads = width // HEAD_DIM
    scale = HEAD_DIM ** (-0.5)
    key_acc[...] = jnp.zeros_like(key_acc)
    value_acc[...] = jnp.zeros_like(value_acc)

    for start in range(0, qkv_ref.shape[0], ATTEND_ROWS):
        if start:
            yield
        rows, distance, allowed = places_of(start, label_col_ref, label_row_ref)
        d_mixed = product(d_branch_ref[rows, :], mats_ref[:, 3 * width :], 1, 0).astype(
            jnp.bfloat16
        )
        queries = qkv_ref[rows, :width]
        d_queries, d_keys, d_values = [], [], []
        for head in range(heads):
            own_queries = head_of(queries, head)
            key_rows = head_of(qkv_ref[:, width : 2 * width], head)
            scores = scores_of(own_queries, key_rows, slope_ref[head : head + 1, :], distance, allowed)
            probs = jnp.exp(scores - logsum_ref[rows, head : head + 1])
            d_own = head_of(d_mixed, head)
            d_probs = product(d_own, head_of(qkv_ref[:, 2 * width :], head), 1, 1)
            inner = jnp.sum(probs * d_probs, axis=1, keepdims=True)
            d_scores = (probs * (d_probs - inner)).astype(jnp.bfloat16)
            d_queries.append(product(d_scores, key_rows, 1, 0))
            d_keys.append(product(d_scores, own_queries, 0, 0))
            d_values.append(product(probs.astype(jnp.bfloat16), d_own, 0, 0))
        d_qkv_ref[rows, :width] = (jnp.concatenate(d_queries, axis=1) * scale).astype(jnp.bfloat16)
        key_acc[...] += jnp.concatenate(d_keys, axis=1)
        value_acc[...] += jnp.concatenate(d_values, axis=1)

    d_qkv_ref[:, width : 2 * width] = (key_acc[...] * scale).astype(jnp.bfloat16)
    d_qkv_ref[:, 2 * width :] = value_acc[...].astype(jnp.bfloat16)
    bias_ref[...] = jnp.sum(d_qkv_ref[...].astype(jnp.float32), axis=0, keepdims=True)


def d_normed_kernel(d_qkv_ref, mats_ref, partial_ref):
    width = d_qkv_ref.shape[1] // 3

    @pl.loop(0, partial_ref.shape[0], step=ATTEND_ROWS)
    def _(start):
        rows = pl.ds(pl.multiple_of(start, ATTEND_ROWS), ATTEND_ROWS)
        partial_ref[rows, :] = product(
            d_qkv_ref[rows, :], mats_ref[:, : 3 * width], 1, 1
        ).astype(jnp.bfloat16)


def product(left, right, left_dim, right_dim):
    return lax.dot_general(
        left, right, (((left_dim,), (right_dim,)), ((), ())), preferred_element_type=jnp.float32
    )


GELU_SCALE = (2.0 / 3.141592653589793) ** 0.5
GELU_CUBE = 0.044715


class Flat:
    def __init__(self, ref):
        self.ref = ref

    def __getitem__(self, key):
        value = self.ref[:, :, :, :, key[1]]
        return value.reshape(-1, value.shape[-1])


class GatherLater(Gather):
    patience = 1


class Sublayer:
    peers = beside("x")
    copies = 12
    spreads = True

    def __init__(self, own, *operands):
        self.count = len(operands)
        group = own.shape[0] * (RING if self.spreads else 1)
        partial = jax.ShapeDtypeStruct((group, own.shape[1]), jnp.bfloat16)
        self.spread, self.fold = Spread(own), Fold(partial)
        self.extra = tuple(
            jax.ShapeDtypeStruct(*shape) for shape in self.results(group, *operands)
        )
        self.own_scratch = self.work(group, *operands)
        self.out = (self.fold.out,) + ((self.spread.out,) if self.spreads else ()) + self.extra
        self.scratch = (
            [pltpu.VMEM(partial.shape, partial.dtype)]
            + (self.spread.scratch if self.spreads else [])
            + self.fold.scratch
            + self.own_scratch
        )

    def work(self, group, *operands):
        return []

    def before(self, lanes, operands, extra, work):
        return []

    def after(self, lanes, rows, operands, extra, work):
        return []

    def steps(self, lanes, own_ref, *refs):
        self.lanes = lanes
        refs = list(refs)
        operands, refs = refs[: self.count], refs[self.count :]
        total_ref = refs.pop(0)
        rows_ref = refs.pop(0) if self.spreads else own_ref
        extra, refs = refs[: len(self.extra)], refs[len(self.extra) :]
        partial_ref = refs.pop(0)
        keep = [refs.pop(0)] if self.spreads else []
        mixing, work = refs[:3], refs[3:]
        if self.spreads:
            self.spread.early, self.spread.late = self.early, self.late
            yield from weave(
                self.spread.steps(lanes, own_ref, rows_ref, *keep),
                *self.before(lanes, operands, extra, work),
            )
        yield from self.compute(rows_ref, operands, extra, partial_ref, work)
        yield from weave(
            self.fold.steps(lanes, partial_ref, total_ref, *mixing),
            *self.after(lanes, rows_ref, operands, extra, work),
        )


class Attend(Sublayer):
    def results(self, group, mats, bias, *rest):
        width = bias.shape[1] // 3
        return (
            ((group, 3 * width), jnp.bfloat16),
            ((group, width // HEAD_DIM), jnp.float32),
            ((group, width), jnp.bfloat16),
        )

    def compute(self, rows, operands, extra, partial, work):
        attend_kernel(rows, *operands, *extra, partial)
        yield from ()


class AttendFirst(Attend):
    peers = list(dict.fromkeys(Sublayer.peers + Gather.peers))
    copies = Sublayer.copies + Gather.copies

    def results(self, group, shard, bias, *rest):
        self.gather = Gather(shard)
        return super().results(group, shard, bias, *rest) + (
            (self.gather.out.shape, self.gather.out.dtype),
        )

    def before(self, lanes, operands, extra, work):
        return [self.gather.steps(lanes, operands[0], extra[-1])]

    def compute(self, rows, operands, extra, partial, work):
        attend_kernel(rows, Flat(extra[-1]), *operands[1:], *extra[:-1], partial)
        yield from ()


class AttendBack(Sublayer):
    def results(self, group, mats, qkv, *rest):
        return (qkv.shape, jnp.bfloat16), ((1, qkv.shape[1]), jnp.float32)

    def work(self, group, mats, qkv, *rest):
        return [pltpu.VMEM((group, qkv.shape[1] // 3), jnp.float32)] * 2

    def compute(self, rows, operands, extra, partial, work):
        yield from attend_back_kernel(
            rows, *operands[:6], extra[0], extra[1], *work[:2]
        )
        self.start(rows, operands, extra, work)
        d_normed_kernel(extra[0], operands[0], partial)


    def start(self, rows, operands, extra, work):
        pass


class AttendBackFirst(AttendBack):
    peers = list(dict.fromkeys(Sublayer.peers + Share.peers))
    copies = Sublayer.copies + ShareWhole.copies

    def results(self, group, mats, qkv, *rest):
        normed, attended = rest[-2:]
        self.share = ShareHeads(normed, qkv, normed, attended)
        return super().results(group, mats, qkv) + ((self.share.out.shape, self.share.out.dtype),)

    def work(self, group, mats, qkv, *rest):
        return super().work(group, mats, qkv) + self.share.scratch

    def start(self, rows, operands, extra, work):
        normed, attended = operands[-2:]
        self.sharing = self.share.steps(
            self.lanes, normed, extra[0], rows, attended, extra[2], *work[2:]
        )
        next(self.sharing)

    def after(self, lanes, rows, operands, extra, work):
        return [self.sharing]


class Mlp(Sublayer):
    def results(self, group, mats, bias):
        shape = (group, bias.shape[1])
        return (shape, jnp.float32), (shape, jnp.bfloat16)

    def compute(self, rows_ref, operands, extra, partial_ref, work):
        mats_ref, bias_ref = operands
        pre_ref, hidden_ref = extra
        width = bias_ref.shape[1]

        @pl.loop(0, rows_ref.shape[0], step=ATTEND_ROWS)
        def _(start):
            rows = pl.ds(pl.multiple_of(start, ATTEND_ROWS), ATTEND_ROWS)
            pre = product(rows_ref[rows, :], mats_ref[:, :width], 1, 0) + bias_ref[...]
            pre_ref[rows, :] = pre
            bend = jnp.tanh(GELU_SCALE * (pre + GELU_CUBE * pre * pre * pre))
            hidden = (0.5 * pre * (1.0 + bend)).astype(jnp.bfloat16)
            hidden_ref[rows, :] = hidden
            partial_ref[rows, :] = product(hidden, mats_ref[:, width:], 1, 1).astype(jnp.bfloat16)

        yield from ()


class MlpBackFirst(Sublayer):
    def results(self, group, mats, pre):
        return (pre.shape, jnp.bfloat16), ((1, pre.shape[1]), jnp.float32)

    def compute(self, rows_ref, operands, extra, partial_ref, work):
        mats_ref, pre_ref = operands
        d_pre_ref, sums_ref = extra
        width = pre_ref.shape[1]
        sums_ref[...] = jnp.zeros_like(sums_ref)

        @pl.loop(0, rows_ref.shape[0], step=ATTEND_ROWS)
        def _(start):
            rows = pl.ds(pl.multiple_of(start, ATTEND_ROWS), ATTEND_ROWS)
            d_hidden = product(rows_ref[rows, :], mats_ref[:, width:], 1, 0)
            pre = pre_ref[rows, :]
            square = pre * pre
            bend = jnp.tanh(GELU_SCALE * (pre + GELU_CUBE * pre * square))
            slope = 0.5 * (1.0 + bend) + 0.5 * GELU_SCALE * pre * (1.0 - bend * bend) * (
                1.0 + 3.0 * GELU_CUBE * square
            )
            d_pre = (d_hidden * slope).astype(jnp.bfloat16)
            d_pre_ref[rows, :] = d_pre
            sums_ref[...] += jnp.sum(d_pre.astype(jnp.float32), axis=0, keepdims=True)
            partial_ref[rows, :] = product(d_pre, mats_ref[:, :width], 1, 1).astype(jnp.bfloat16)

        yield from ()


class MlpBack(MlpBackFirst):
    spreads = False
    copies = 6


def attend_operands(vec_rows, masks, tensor_pos, width):
    bias_qkv = jnp.concatenate(
        [
            local_slice(vec_rows[2], tensor_pos, width),
            jnp.zeros((width,), jnp.float32),
            local_slice(vec_rows[3], tensor_pos, width),
        ]
    )
    return (bias_qkv[None],) + masks


def low_norm(values, gain, shift):
    return layer_norm(values, gain, shift).astype(jnp.bfloat16)


def mlp_bias(vec_rows, tensor_pos, width):
    return local_slice(vec_rows[8:], tensor_pos, width).reshape(1, -1)


def norm_back(d_normed, values, gain, shift):
    unused, pull = jax.vjp(layer_norm, values, gain, shift)
    return pull(d_normed)


def vector_grads(gains_a, bias_sums, d_branch, gains_b, d_two, up_sums, tensor_pos):
    width = bias_sums.shape[1] // 3
    head_rows = jnp.stack(
        [
            *gains_a,
            spread_local(bias_sums[0, :width], tensor_pos),
            spread_local(bias_sums[0, 2 * width :], tensor_pos),
            jnp.sum(d_branch.astype(jnp.float32), axis=0),
            *gains_b,
            jnp.sum(d_two.astype(jnp.float32), axis=0),
        ]
    )
    return jnp.concatenate([head_rows, spread_local(up_sums.reshape(-1, width), tensor_pos)])


def on_device(
    tokens,
    cotangent,
    matrices,
    vectors,
    first_moment,
    second_moment,
    momenta,
    lengths,
    assign,
    owner_slots,
):
    dp_pos = lax.axis_index(DP)
    tensor_pos = lax.axis_index("x")
    tok_rows = tokens.shape[0]
    group_rows = tok_rows * lax.axis_size("x")
    total_rows = group_rows * lax.axis_size(DP)
    labels = segment_labels(lengths, assign, dp_pos, group_rows)
    own_labels = lax.dynamic_slice_in_dim(labels, tensor_pos * tok_rows, tok_rows)
    width = matrices.shape[3]
    head_count = width // HEAD_DIM
    head_ids = tensor_pos * head_count + lax.iota(jnp.int32, head_count) + 1
    slopes = 2.0 ** (-8.0 * head_ids.astype(jnp.float32) / HEADS)
    low_mats = matrices.astype(jnp.bfloat16)
    grad_rows = cotangent * (own_labels > 0).astype(jnp.float32)[:, None]
    shards = [(side_by_side(layer[:4]), side_by_side(layer[4:])) for layer in low_mats]
    masks = (labels[:, None], labels[None], slopes[:, None])
    first, second = vectors[0], vectors[1]

    heads = attend_operands(first, masks, tensor_pos, width)
    branch, normed_a0, qkv0, logsum0, attended0, mats_a0, mats_m0 = ride(
        "attend_first",
        (AttendFirst, (low_norm(tokens, first[0], first[1]), shards[0][0]) + heads),
        (GatherLater, shards[0][1]),
        late=1,
    )
    mats_a0, mats_m0 = full_weights(mats_a0), full_weights(mats_m0)
    middle0 = tokens + (branch + first[4])
    branch, normed_b0, pre0, hidden0, mats_a1 = ride(
        "mlp_first",
        (Mlp, (low_norm(middle0, first[5], first[6]), mats_m0, mlp_bias(first, tensor_pos, width))),
        (Gather, shards[1][0]),
        late=1,
    )
    mats_a1 = full_weights(mats_a1)
    resid1 = middle0 + (branch + first[7])
    heads = attend_operands(second, masks, tensor_pos, width)
    grad_out = cotangent * (own_labels > 0).astype(jnp.float32)[:, None]
    d_two1 = grad_out.astype(jnp.bfloat16)
    d_two_all1, branch, normed_a1, qkv1, logsum1, attended1, mats_m1 = ride(
        "attend",
        (SpreadLater, d_two1),
        (Attend, (low_norm(resid1, second[0], second[1]), mats_a1) + heads),
        (Gather, shards[1][1]),
        late=1,
    )
    mats_m1 = full_weights(mats_m1)
    middle1 = resid1 + (branch + second[4])
    branch, normed_b1, pre1, hidden1 = ride(
        "mlp",
        (
            Mlp,
            (low_norm(middle1, second[5], second[6]), mats_m1, mlp_bias(second, tensor_pos, width)),
        ),
    )
    resid = middle1 + (branch + second[7])

    d_normed, d_pre1, up_sums1 = ride("mlp_back", (MlpBack, (d_two_all1, mats_m1, pre1)))
    d_norm, *gains_b1 = norm_back(d_normed, middle1, second[5], second[6])
    d_middle1 = grad_out + d_norm
    d_branch1 = d_middle1.astype(jnp.bfloat16)
    d_normed, d_branch_all1, d_qkv1, bias_sums1, own_m1 = ride(
        "attend_back",
        (AttendBack, (d_branch1, mats_a1, qkv1, logsum1) + masks),
        (ShareMlp, (normed_b1, d_pre1, d_two_all1, hidden1)),
    )
    d_norm, *gains_a1 = norm_back(d_normed, resid1, second[0], second[1])
    grad_mid = d_middle1 + d_norm
    d_two0 = grad_mid.astype(jnp.bfloat16)
    d_normed, d_two_all0, d_pre0, up_sums0, own_a1 = ride(
        "mlp_back_first",
        (MlpBackFirst, (d_two0, mats_m0, pre0)),
        (ShareHeads, (normed_a1, d_qkv1, d_branch_all1, attended1)),
    )
    d_norm, *gains_b0 = norm_back(d_normed, middle0, first[5], first[6])
    d_middle0 = grad_mid + d_norm
    d_branch0 = d_middle0.astype(jnp.bfloat16)
    d_normed, d_branch_all0, d_qkv0, bias_sums0, own_a0, own_m0 = ride(
        "attend_back_first",
        (
            AttendBackFirst,
            (d_branch0, mats_a0, qkv0, logsum0) + masks + (normed_a0, attended0),
        ),
        (ShareMlp, (normed_b0, d_pre0, d_two_all0, hidden0)),
    )
    d_norm, *gains_a0 = norm_back(d_normed, tokens, first[0], first[1])
    grad_rows = d_middle0 + d_norm
    vec_first = vector_grads(
        gains_a0, bias_sums0, d_branch0, gains_b0, d_two0, up_sums0, tensor_pos
    )
    vec_second = vector_grads(
        gains_a1, bias_sums1, d_branch1, gains_b1, d_two1, up_sums1, tensor_pos
    )
    own_grads = [own_a0, own_m0, own_a1, own_m1]
    low_grads = jnp.concatenate(
        [split_units(own, blocks) for own, blocks in zip(own_grads, (4, 2, 4, 2))], axis=0
    )
    grad_matrices = low_grads.astype(jnp.float32).reshape(matrices.shape)
    slot_count = momenta.shape[0] * lax.axis_size(DP)
    one_hot = (owner_slots[None, :] == lax.iota(jnp.int32, slot_count)[:, None]).astype(
        jnp.bfloat16
    )
    outgoing = jnp.einsum(
        "su,urc->src", one_hot, low_grads, preferred_element_type=jnp.float32
    ).astype(jnp.bfloat16)
    new_momenta, moment, grad_vectors = ride(
        "moments",
        (Moments, (outgoing, momenta[0])),
        (Total, jnp.concatenate([vec_first, vec_second]).reshape(8, 8, 384)),
    )
    new_momenta = new_momenta[None]
    current, squares = orthogonal(moment, width)
    momentum_scales = jnp.sqrt(squares[0, 0:1]) / (float(total_rows) ** 0.5 * D)
    returned = ride("returns", (Returns, current.reshape(outgoing.shape)))[0]
    grad_vectors = grad_vectors.reshape(vectors.shape)
    new_first = ADAM_FIRST * first_moment + (1.0 - ADAM_FIRST) * grad_vectors
    new_second = ADAM_SECOND * second_moment + (1.0 - ADAM_SECOND) * grad_vectors * grad_vectors
    first_fix = 1.0 - ADAM_FIRST**STEP
    second_fix = 1.0 - ADAM_SECOND**STEP
    new_vectors = vectors - VECTOR_RATE * (new_first / first_fix) / (
        jnp.sqrt(new_second / second_fix) + ADAM_EPSILON
    )
    unit_steps = jnp.einsum("su,src->urc", one_hot, returned, preferred_element_type=jnp.float32)
    new_matrices = matrices - MUON_RATE * unit_steps.reshape(matrices.shape)
    return (
        resid,
        grad_rows,
        grad_matrices,
        new_matrices,
        new_momenta,
        grad_vectors,
        new_first,
        new_second,
        new_vectors,
        momentum_scales,
    )


def solution(mesh):
    fine = Mesh(mesh.devices.reshape(4, 4, 2, RING), ALL)
    rows = P(ALL, None)
    shards = P(None, None, DP, "x")
    slots = P(DP, None, "x")
    return jax.shard_map(
        on_device,
        mesh=fine,
        in_specs=(rows, rows, shards, P(), P(), P(), slots, P(), P(), P()),
        out_specs=(rows, rows, shards, shards, slots, P(), P(), P(), P(), P(DP)),
        check_vma=False,
    )
```
